32 devices in a mesh: dp: 4 (over z), seq: 2 (over core), expert: 4 (over y, x).
Axes of the slice: x: 2, y: 2, z: 4, core: 2. Of those that a mesh axis runs over, the one named last changes fastest.
Arguments:
- keys: bfloat16 [4, 1024, 512], P('expert', ('dp', 'seq')), may hold values from -4 to 4
- values: bfloat16 [4, 1024, 512], P('expert', ('dp', 'seq')), may hold values from -5 to 5
- queries: bfloat16 [4, 8, 4096], P('expert', ('dp', 'seq')), may hold values from -80 to 80
- residual: bfloat16 [4, 8, 2048], P('expert', ('dp', 'seq')), may hold values from -9 to 9
- out_proj: bfloat16 [4096, 2048], P(('dp', 'seq')), may hold values from -0.09375 to 0.09375
- norm_gain: bfloat16 [2048], replicated, may hold values from 0.25 to 1.75
- router: bfloat16 [2048, 16], replicated, may hold values from -8 to 8
- w_gate: bfloat16 [16, 2048, 768], P(('dp', 'expert'), None, 'seq'), may hold values from -0.125 to 0.125
- w_up: bfloat16 [16, 2048, 768], P(('dp', 'expert'), None, 'seq'), may hold values from -0.125 to 0.125
- w_down: bfloat16 [16, 768, 2048], P(('dp', 'expert'), 'seq'), may hold values from -0.21875 to 0.21875
- head_vec: bfloat16 [2048], replicated, may hold values from -0.09 to 0.09
- routes: int32 [4, 8, 8], P('expert', 'dp'), may hold values from 0 to 15, all different within a row; in each aligned block of 2 rows (0 to 1, 2 to 3, ..., all dimensions but the last counted through in order) at most 2 rows name the same one
- step_pos: int32 [4, 8], P('expert'), may hold values from 0 to 1023, as said below
- labels: int32 [4, 8], P('expert', ('dp', 'seq')), may hold values 0 or 1
- trace_len: int32 [4, 8], P('expert'), may hold values from 1 to 256, 1024 in all within a row
Outputs:
- loss: float32 [], replicated
- grad_down: bfloat16 [16, 768, 2048], P(('dp', 'expert'), 'seq')
- grad_router: bfloat16 [2048, 16], P(('dp', 'seq', 'expert'))
The draws below stay inside these ranges and needn't reach their ends.
Inputs may be any that keep to these rules, and one draw needn't show every extreme that they name: `step_pos`: increasing along each pack; distinct. `routes`: in each aligned block of 2 step ends (those of one index of dp in one pack) no expert is named by more than 2 of them.
All inputs are finite; a program needn't handle non-finite values. No bound on the sum of `labels` on one device may be relied on, other than what follows from the above.
Results may differ from the reference program's by a relative error of at most 0.018.
Values may be sent and summed in bfloat16 or wider, within the bound.
A program may use at most 64 MiB of HBM per device.

```python
import math
import jax
import jax.numpy as jnp
import numpy as np
from jax import lax

D = 2048
QUERY_HEADS = 32
KEY_VALUE_HEADS = 4
HEAD_WIDTH = 128
FF = 768
TOPK = 8
TRACES = 8
TOK_DEV = 128
PACK_COUNT = 4
PACK_TOKENS = 1024
STEPS = 8
EXPERTS = 16
BLOCK = 2
CAP = 2


def step_positions(key):
    window = min(PACK_TOKENS, max(2 * STEPS, TOK_DEV))
    forced = jax.random.randint(jax.random.fold_in(key, 5), (), 0, PACK_COUNT)
    coins = jax.random.randint(jax.random.fold_in(key, 6), (PACK_COUNT,), 0, 2)
    clustered = (coins == 1) | (jnp.arange(PACK_COUNT) == forced)

    def one_pack(pack_number):
        pack_key = jax.random.fold_in(key, pack_number)
        spread_out = jnp.sort(jax.random.permutation(pack_key, PACK_TOKENS)[:STEPS]).astype(jnp.int32)
        offset = jax.random.randint(jax.random.fold_in(pack_key, 71), (), 0, PACK_TOKENS - window + 1)
        inside = jnp.sort(jax.random.permutation(jax.random.fold_in(pack_key, 73), window)[:STEPS]).astype(jnp.int32)
        packed_close = (inside + offset).astype(jnp.int32)
        return jnp.where(clustered[pack_number], packed_close, spread_out).astype(jnp.int32)
    return jax.vmap(one_pack)(jnp.arange(PACK_COUNT))


def draw_step_pos(key, part):
    return step_positions(jax.random.fold_in(key, 11))


def draw_keys(key, part):
    gaussian_portion = jax.random.normal(jax.random.fold_in(key, 23), (PACK_COUNT, PACK_TOKENS, KEY_VALUE_HEADS * HEAD_WIDTH), jnp.float32)
    gaussian_portion = jnp.clip(gaussian_portion, -4.0, 4.0)
    return gaussian_portion.astype(jnp.bfloat16)


def draw_queries(key, part):
    gaussian_portion = jax.random.normal(jax.random.fold_in(key, 37), (PACK_COUNT, STEPS, QUERY_HEADS * HEAD_WIDTH), jnp.float32)
    gaussian_portion = jnp.clip(gaussian_portion, -5.0, 5.0)
    return gaussian_portion.astype(jnp.bfloat16)


def draw_router(key, part):
    spread = D ** (-0.5)
    gaussian_portion = jax.random.normal(jax.random.fold_in(key, 53), (D, EXPERTS), jnp.float32) * spread
    gaussian_portion = jnp.clip(gaussian_portion, -6.0 * spread, 6.0 * spread)
    return gaussian_portion.astype(jnp.bfloat16)


def head_direction(key):
    direction = jax.random.normal(jax.random.fold_in(key, 91), (D,), jnp.float32)
    return jnp.clip(direction, -3.0, 3.0)


def draw_head_vec(key, part):
    return (0.03 * head_direction(key)).astype(jnp.bfloat16)


def draw_residual(key, part):
    noise = jax.random.normal(jax.random.fold_in(key, 97), (PACK_COUNT, STEPS, D), jnp.float32)
    noise = jnp.clip(noise, -5.0, 5.0)
    reach = 10.0 / (0.03 * D)
    ramp = jnp.arange(STEPS, dtype=jnp.float32) / max(STEPS - 1, 1)
    direction = head_direction(key)
    combined = noise + reach * ramp[None, :, None] * direction[None, None, :]
    return jnp.clip(combined, -9.0, 9.0).astype(jnp.bfloat16)


def with_ends(result, own_key, smallest, largest):
    spot = [jax.random.randint(jax.random.fold_in(own_key, axis), (), 0, length) for axis, length in enumerate(result.shape)]
    main_axis = result.shape.index(max(result.shape))
    next_to = spot[:main_axis] + [(spot[main_axis] + 1) % result.shape[main_axis]] + spot[main_axis + 1:]
    return result.at[tuple(spot)].set(smallest).at[tuple(next_to)].set(largest)


def block_levels(key, shape, cuts, smallest, top_value):
    loudness = 1.0
    for position, blocks in cuts:
        draws = jax.random.uniform(jax.random.fold_in(jax.random.fold_in(key, 6), position), (blocks,), jnp.float32, smallest / len(cuts), top_value / len(cuts))
        loudness = loudness * jnp.repeat(jnp.exp(draws), shape[position] // blocks).reshape((-1,) + (1,) * (len(shape) - 1 - position))
    return loudness


def length_profile(number_of, total, bound, lean):
    loads = [(1 << 20) // math.isqrt(standing ** lean) + 1 for standing in range(2, number_of + 1)]
    surplus, given = total - bound - (number_of - 1), [1] * (number_of - 1)
    while surplus > 0:
        candidates = [i for i in range(number_of - 1) if given[i] < bound]
        mass, budget = sum([loads[i] for i in candidates]), surplus
        for i in candidates:
            addition = min(bound - given[i], max(1, budget * loads[i] // mass), surplus)
            given[i] = given[i] + addition
            surplus = surplus - addition
    return np.array([bound] + given)


def ragged(key, amount, total, limit, skew):
    if amount == 2:
        one = jax.random.randint(key, (), max(1, total - limit), min(limit, total - 1) + 1)
        return jnp.stack([one, total - one])
    tallies = jnp.asarray(length_profile(amount, total, limit, skew), jnp.int32)
    twos = (amount - 1) // 2
    donor, receiver = tallies[1:1 + 2 * twos:2], tallies[2:2 + 2 * twos:2]
    slack = jnp.minimum(donor - 1, limit - receiver)
    moved = jax.random.randint(jax.random.fold_in(key, 1), (twos,), 0, 1 << 20) % (slack + 1)
    tallies = tallies.at[1:1 + 2 * twos:2].set(donor - moved).at[2:2 + 2 * twos:2].set(receiver + moved)
    return tallies[jax.random.permutation(jax.random.fold_in(key, 2), amount)]


def assign_block(own_key, own, number, rows, count, top, most, skew):
    ranking = jax.random.permutation(own_key, count)
    crowded, common = shares(count, rows * top, most, skew, True), shares(count, rows * top, most, skew, False)
    places = jnp.arange(count)

    def named(sizes, rotation):
        used = int((sizes > 0).sum())
        fixed = max(1, used // 4)
        moved = fixed + (places - fixed + rotation * (used - fixed)) % max(1, count - fixed)
        return jnp.zeros((count,), jnp.int32).at[ranking[jnp.where(places < fixed, places, moved)]].set(jnp.asarray(sizes, jnp.int32))

    sizes = jnp.where(number % 4 == 0, named(crowded, number // 4), named(common, number - number // 4 - 1))
    mixed = jax.random.permutation(jax.random.fold_in(own, 3), count)
    giver, sink = mixed[0:count // 2 * 2:2], mixed[1:count // 2 * 2:2]
    slack = jnp.minimum(sizes[giver] - 1, most - sizes[sink]) // 2
    slack = jnp.where((giver == ranking[0]) | (sink == ranking[0]) | (sizes[sink] == 0), 0, jnp.maximum(slack, 0))
    moved = jax.random.randint(jax.random.fold_in(own, 4), (count // 2,), 0, 1 << 20) % (slack + 1)
    sizes = sizes.at[giver].add(-moved).at[sink].add(moved)
    items = jnp.searchsorted(jnp.cumsum(sizes), jnp.arange(rows * top), side="right").astype(jnp.int32)
    listing = items.reshape(top, rows).T
    listing = listing[jax.random.permutation(jax.random.fold_in(own, 1), rows)]
    rotation = jax.random.randint(jax.random.fold_in(own, 2), (rows, 1), 0, top)
    return jnp.take_along_axis(listing, (jnp.arange(top)[None, :] + rotation) % top, axis=1)


def shares(number_of, total, most, lean, full):
    weights = [(1 << 20) // math.isqrt(standing ** lean) + 1 for standing in range(1, number_of + 1)]
    largest = most if full else min(most, max(-(-total // number_of), total * weights[0] // sum(weights)))
    least = 1 if total - largest >= number_of - 1 else 0
    given, surplus = [largest] + [least] * (number_of - 1), total - largest - least * (number_of - 1)
    while surplus > 0:
        candidates = [i for i in range(1, number_of) if given[i] < largest] or [i for i in range(1, number_of) if given[i] < most]
        pool, remaining = sum([weights[i] for i in candidates]), surplus
        for i in candidates:
            more = min(most - given[i], max(1, remaining * weights[i] // pool), surplus)
            given[i] = given[i] + more
            surplus = surplus - more
    return np.array(given)


def centred(stream_key, extent, width, limit, cuts=(), kind=jnp.bfloat16):
    entries = width * jax.random.normal(stream_key, extent, jnp.float32)
    if cuts:
        entries = entries * block_levels(stream_key, extent, cuts, -0.22, 0.18)
    return jnp.clip(entries, -limit, limit).astype(kind)


def setup_inputs(seed: int = 0) -> dict:
    seeds = jax.random.split(jax.random.key(seed), 16)
    keys = draw_keys(jax.random.fold_in(seeds[15], 71), 0)
    values = centred(seeds[1], (PACK_COUNT, PACK_TOKENS, KEY_VALUE_HEADS * HEAD_WIDTH), 1.0, 5.0, ((0, 4), (1, 8)))
    queries = draw_queries(jax.random.fold_in(seeds[15], 71), 0)
    residual = draw_residual(jax.random.fold_in(seeds[15], 71), 0)
    out_proj = centred(seeds[4], (QUERY_HEADS * HEAD_WIDTH, D), (QUERY_HEADS * HEAD_WIDTH) ** -0.5, 0.09375, ((0, 8),))
    norm_gain = jnp.clip(1.0 + 0.15 * jax.random.normal(seeds[5], (D,), jnp.float32), 0.25, 1.75).astype(jnp.bfloat16)
    router = draw_router(jax.random.fold_in(seeds[15], 71), 0)
    w_gate = centred(seeds[7], (EXPERTS, D, FF), D ** -0.5, 0.125, ((0, 16), (2, 2)))
    w_up = centred(seeds[8], (EXPERTS, D, FF), D ** -0.5, 0.125, ((0, 16), (2, 2)))
    w_down = centred(seeds[9], (EXPERTS, FF, D), FF ** -0.5, 0.21875, ((0, 16), (1, 2)))
    head_vec = draw_head_vec(jax.random.fold_in(seeds[15], 71), 0)
    routes_keys = jax.random.split(jax.random.fold_in(seeds[11], 1), PACK_COUNT * STEPS // BLOCK)
    routes_turns = jax.random.permutation(jax.random.fold_in(seeds[11], 3), PACK_COUNT * STEPS // BLOCK)
    routes = jax.vmap(lambda own, number: assign_block(jax.random.fold_in(seeds[11], 2), own, number, BLOCK, EXPERTS, TOPK, CAP, 2))(routes_keys, routes_turns).reshape((PACK_COUNT, STEPS, TOPK))
    step_pos = draw_step_pos(jax.random.fold_in(seeds[15], 71), 0)
    labels = with_ends((jax.random.randint(seeds[13], (PACK_COUNT, STEPS), 0, 2) < 1).astype(jnp.int32), jax.random.fold_in(seeds[13], 1), 0, 1)
    trace_len = jax.vmap(lambda own: ragged(own, TRACES, PACK_TOKENS, PACK_TOKENS // 4, 2))(jax.random.split(seeds[14], PACK_COUNT)).reshape((PACK_COUNT, TRACES)).astype(jnp.int32)
    return dict(keys=keys, values=values, queries=queries, residual=residual, out_proj=out_proj, norm_gain=norm_gain, router=router, w_gate=w_gate, w_up=w_up, w_down=w_down, head_vec=head_vec, routes=routes, step_pos=step_pos, labels=labels, trace_len=trace_len)


MASKED = -1e+30
EPSILON = 1e-06

def rms_scale(stream):
    return lax.rsqrt(lax.optimization_barrier(jnp.mean(stream * stream, axis=-1, keepdims=True)) + EPSILON)

def attend(packed):
    pack_keys, pack_values, pack_queries, positions, lengths = packed
    trace_ends = jnp.cumsum(lengths)
    starts = lax.optimization_barrier(jnp.sum(jnp.where(trace_ends[None, :] <= positions[:, None], lengths[None, :], 0), axis=1))
    key_pos = jnp.arange(PACK_TOKENS, dtype=jnp.int32)
    allowed = (key_pos[None, :] <= positions[:, None]) & (key_pos[None, :] >= starts[:, None])
    query_groups = QUERY_HEADS // KEY_VALUE_HEADS
    results = []
    for head_cluster in range(KEY_VALUE_HEADS):
        query_part = pack_queries[:, head_cluster * query_groups * HEAD_WIDTH:(head_cluster + 1) * query_groups * HEAD_WIDTH].reshape(STEPS * query_groups, HEAD_WIDTH)
        key_part = pack_keys[:, head_cluster * HEAD_WIDTH:(head_cluster + 1) * HEAD_WIDTH]
        value_part = pack_values[:, head_cluster * HEAD_WIDTH:(head_cluster + 1) * HEAD_WIDTH]
        scores = jnp.dot(query_part, key_part.T, preferred_element_type=jnp.float32) * HEAD_WIDTH ** (-0.5)
        scores = scores.reshape(STEPS, query_groups, PACK_TOKENS)
        scores = jnp.where(allowed[:, None, :], scores, MASKED)
        peak_score = lax.optimization_barrier(jnp.max(scores, axis=2, keepdims=True))
        complete_weight_rows = jnp.where(allowed[:, None, :], jnp.exp(scores - peak_score), 0.0)
        totals = lax.optimization_barrier(jnp.sum(complete_weight_rows, axis=2, keepdims=True))
        weighted = jnp.dot(complete_weight_rows.astype(jnp.bfloat16).reshape(STEPS * query_groups, PACK_TOKENS), value_part, preferred_element_type=jnp.float32).reshape(STEPS, query_groups, HEAD_WIDTH)
        results.append(weighted / totals)
    return jnp.stack(results, axis=1).reshape(STEPS, QUERY_HEADS * HEAD_WIDTH).astype(jnp.bfloat16)

def head_logit(final, head_vec):
    return lax.optimization_barrier(jnp.sum(final * rms_scale(final) * head_vec.astype(jnp.float32)[None, :], axis=1))

def reference(keys, values, queries, residual, out_proj, norm_gain, router, w_gate, w_up, w_down, head_vec, routes, step_pos, labels, trace_len):
    attn = lax.map(attend, (keys, values, queries, step_pos, trace_len))
    row_count = PACK_COUNT * STEPS
    mixed = jnp.dot(attn.reshape(row_count, QUERY_HEADS * HEAD_WIDTH), out_proj, preferred_element_type=jnp.float32)
    stream = residual.reshape(row_count, D).astype(jnp.float32) + mixed
    normed = (stream * rms_scale(stream) * norm_gain.astype(jnp.float32)[None, :]).astype(jnp.bfloat16)
    logits = jnp.dot(normed, router, preferred_element_type=jnp.float32)
    route_ids = routes.reshape(row_count, TOPK)
    chosen = (route_ids[:, :, None] == jnp.arange(EXPERTS, dtype=jnp.int32)[None, None, :]).astype(jnp.float32)
    picked = lax.optimization_barrier(jnp.sum(chosen * logits[:, None, :], axis=2))
    gate_weight = jax.nn.softmax(picked, axis=-1)
    block_count = row_count // BLOCK
    flat_routes = route_ids.reshape(block_count, BLOCK * TOPK)
    onehot = (flat_routes[:, :, None] == jnp.arange(EXPERTS, dtype=jnp.int32)[None, None, :]).astype(jnp.int32)
    order_rank = lax.optimization_barrier(jnp.sum((jnp.cumsum(onehot, axis=1) - 1) * onehot, axis=2))
    slot_index = (jnp.arange(block_count, dtype=jnp.int32)[:, None] * CAP + order_rank).reshape(-1).astype(jnp.int32)
    destination = route_ids.reshape(-1)
    row_of = jnp.repeat(jnp.arange(row_count, dtype=jnp.int32), TOPK)
    span = block_count * CAP
    row_buffer = jnp.zeros((EXPERTS, span, D), jnp.bfloat16).at[destination, slot_index].set(normed[row_of])

    def expert_forward(packed):
        rows_e, gate_e, up_e, down_e = packed
        gate_act = jnp.dot(rows_e, gate_e, preferred_element_type=jnp.float32)
        up_act = jnp.dot(rows_e, up_e, preferred_element_type=jnp.float32)
        hidden = (jax.nn.silu(gate_act) * up_act).astype(jnp.bfloat16)
        return (hidden, jnp.dot(hidden, down_e, preferred_element_type=jnp.float32))
    hidden, out_buffer = lax.map(expert_forward, (row_buffer, w_gate, w_up, w_down))
    expert_out = out_buffer[destination, slot_index].reshape(row_count, TOPK, D)
    expert_mix = lax.optimization_barrier(jnp.sum(gate_weight[:, :, None] * expert_out, axis=1))
    final = stream + expert_mix
    reward, pull = jax.vjp(lambda value: head_logit(value, head_vec), final)
    target = labels.reshape(row_count).astype(jnp.float32)
    loss = jnp.sum(jax.nn.softplus(reward) - target * reward)
    logit_grad = jax.nn.sigmoid(reward) - target
    final_grad, = pull(logit_grad)
    d_mix = final_grad.astype(jnp.bfloat16)
    route_dot = lax.optimization_barrier(jnp.sum(d_mix.astype(jnp.float32)[:, None, :] * expert_out, axis=2))
    pick_grad = gate_weight * (route_dot - lax.optimization_barrier(jnp.sum(gate_weight * route_dot, axis=1, keepdims=True)))
    d_logits = lax.optimization_barrier(jnp.sum(chosen * pick_grad[:, :, None], axis=1))
    grad_router = jnp.dot(normed.astype(jnp.float32).T, d_logits, precision=lax.Precision.HIGHEST).astype(jnp.bfloat16)
    d_out = (gate_weight[:, :, None] * d_mix.astype(jnp.float32)[:, None, :]).astype(jnp.bfloat16).reshape(row_count * TOPK, D)
    grad_buffer = jnp.zeros((EXPERTS, span, D), jnp.bfloat16).at[destination, slot_index].set(d_out)

    def down_grad(packed):
        hidden_e, grads_e = packed
        return jnp.dot(hidden_e.T, grads_e, preferred_element_type=jnp.float32).astype(jnp.bfloat16)
    grad_down = lax.map(down_grad, (hidden, grad_buffer))
    return (loss, grad_down, grad_router)
```

```python
import functools

import jax
import jax.numpy as jnp
from jax import lax
from jax.experimental import pallas as pl
from jax.experimental.pallas import tpu as pltpu
from jax.sharding import PartitionSpec as P

QUERY_HEADS = 32
KEY_VALUE_HEADS = 4
HEAD_WIDTH = 128
LANES = 128
MASKED = -1e30
EPSILON = 1e-06
MESH = pl.DeviceIdType.MESH
F32 = jnp.float32
BF16 = jnp.bfloat16


def iota(shape, axis):
    return lax.broadcasted_iota(jnp.int32, shape, axis)


def total(x):
    return jnp.sum(jnp.sum(x, axis=1, keepdims=True), axis=0, keepdims=True)


def to_row(column, n):
    eye = iota((n, n), 0) == iota((n, n), 1)
    return jnp.sum(jnp.where(eye, column, 0.0), axis=0, keepdims=True)


def to_column(row, n):
    eye = iota((n, n), 0) == iota((n, n), 1)
    return jnp.sum(jnp.where(eye, row, 0.0), axis=1, keepdims=True)


def kernel(
    sizes,
    keys,
    values,
    queries,
    residual,
    out_proj,
    gain,
    router,
    w_gate,
    w_up,
    w_down,
    head,
    routes,
    step_pos,
    labels,
    trace_len,
    loss_out,
    hidden_out,
    grads_out,
    router_out,
    key_v,
    value_v,
    proj_v,
    gate_v,
    up_v,
    down_v,
    q_own,
    q_buf,
    q_f32,
    part_send,
    part_buf,
    stat_send,
    stat_buf,
    mix_f32,
    mix_send,
    mix_buf,
    norm_own,
    norm_buf,
    norm_f32,
    rows,
    out_f32,
    out_send,
    out_buf,
    grad_send,
    grad_buf,
    grad_f32,
    dlog_own,
    dlog_buf,
    load_sem,
    send_sem,
    recv_sem,
):
    DP, SQ, EN = sizes
    G, E = DP * SQ, DP * EN
    N = G * EN
    width = residual.shape[1]
    WB = width // LANES
    dp, sq, ex = lax.axis_index("dp"), lax.axis_index("seq"), lax.axis_index("expert")
    mine = dp * SQ + sq
    me = ex * G + mine
    tokens = keys.shape[1]

    loads = [
        pltpu.make_async_copy(source.at[0] if cut else source, target, load_sem.at[i])
        for i, (source, target, cut) in enumerate(
            [
                (keys, key_v, True),
                (values, value_v, True),
                (out_proj, proj_v, False),
                (w_gate, gate_v, True),
                (w_up, up_v, True),
                (w_down, down_v, True),
            ]
        )
    ]
    for load in loads:
        load.start()

    def device(t):
        place = lax.rem(t, G)
        return (place // SQ, lax.rem(place, SQ), t // G)

    barrier = pltpu.get_barrier_semaphore()

    def greet(i, carry):
        pl.semaphore_signal(
            barrier, inc=1, device_id=device(lax.rem(me + i, N)), device_id_type=MESH
        )
        return carry

    lax.fori_loop(1, N, greet, 0)

    def send(source, target, number, to):
        pltpu.make_async_remote_copy(
            src_ref=source,
            dst_ref=target,
            send_sem=send_sem.at[number],
            recv_sem=recv_sem.at[number],
            device_id=to,
            device_id_type=MESH,
        ).start()

    def to_pack(body):
        def step(i, carry):
            place = lax.rem(mine + i, G)
            body(place, (place // SQ, lax.rem(place, SQ), ex))
            return carry

        lax.fori_loop(1, G, step, 0)

    def to_all(body):
        def step(i, carry):
            t = lax.rem(me + i, N)
            body(t, device(t))
            return carry

        lax.fori_loop(1, N, step, 0)

    def await_all(buf, count, sem):
        span = buf.at[pl.ds(0, count)]
        pltpu.make_async_copy(span, span, sem).wait()

    q_row = queries[...].astype(F32)
    q_own[...] = jnp.concatenate(
        [q_row[:, h * LANES : (h + 1) * LANES] for h in range(QUERY_HEADS)], axis=0
    ).astype(BF16)

    traces = trace_len.shape[1]
    pos_col = to_column(step_pos[...].astype(F32), G)
    len_row = trace_len[...].astype(F32)
    len_col = to_column(len_row, traces)
    before = iota((traces, traces), 0) <= iota((traces, traces), 1)
    ends_row = jnp.sum(jnp.where(before, len_col, 0.0), axis=0, keepdims=True)
    start_col = jnp.sum(jnp.where(ends_row <= pos_col, len_row, 0.0), axis=1, keepdims=True)
    key_pos = (mine * tokens + iota((G, tokens), 1)).astype(F32)
    allowed = jnp.where((key_pos <= pos_col) & (key_pos >= start_col), 1.0, 0.0)
    group = QUERY_HEADS // KEY_VALUE_HEADS
    allowed = jnp.concatenate([allowed] * group, axis=0) > 0.5

    pl.semaphore_wait(barrier, N - 1)

    to_pack(lambda place, to: send(q_own, q_buf.at[mine], 0, to))
    q_buf[mine] = q_own[...]
    loads[0].wait()
    loads[1].wait()
    await_all(q_buf, G - 1, recv_sem.at[0])

    q_f32[...] = q_buf[...].astype(F32).reshape(G * QUERY_HEADS, LANES)
    peaks, sums = [], []
    per_group = KEY_VALUE_HEADS
    owners = G // per_group
    for g in range(KEY_VALUE_HEADS):
        q_part = jnp.concatenate(
            [q_f32[pl.ds(g * group + h, G, stride=QUERY_HEADS), :] for h in range(group)], axis=0
        ).astype(BF16)
        columns = slice(g * HEAD_WIDTH, (g + 1) * HEAD_WIDTH)
        score = (
            lax.dot_general(
                q_part, key_v[:, columns], (((1,), (1,)), ((), ())), preferred_element_type=F32
            )
            * HEAD_WIDTH ** (-0.5)
        )
        score = jnp.where(allowed, score, MASKED)
        peak = jnp.max(score, axis=1, keepdims=True)
        weight = jnp.where(allowed, jnp.exp(score - peak), 0.0)
        peaks.append(peak)
        sums.append(jnp.sum(weight, axis=1, keepdims=True))
        part = jnp.dot(weight.astype(BF16), value_v[:, columns], preferred_element_type=F32)
        part_send[g * owners : (g + 1) * owners] = part.astype(BF16).reshape(
            owners, QUERY_HEADS, LANES
        )
    peaks, sums = jnp.concatenate(peaks, axis=0), jnp.concatenate(sums, axis=0)
    for b in range(G * QUERY_HEADS // LANES):
        span = slice(b * LANES, (b + 1) * LANES)
        stat_send[b] = jnp.concatenate(
            [to_row(peaks[span], LANES), to_row(sums[span], LANES), jnp.zeros((6, LANES), F32)],
            axis=0,
        )
    per_block = LANES // QUERY_HEADS

    def send_parts(place, to):
        send(stat_send.at[place // per_block], stat_buf.at[mine], 2, to)
        send(part_send.at[place], part_buf.at[mine], 1, to)

    to_pack(send_parts)
    part_buf[mine] = part_send[mine]
    stat_buf[mine] = stat_send[mine // per_block]
    loads[2].wait()
    await_all(stat_buf, G - 1, recv_sem.at[2])
    await_all(part_buf, G - 1, recv_sem.at[1])

    lane = iota((QUERY_HEADS, LANES), 1)
    pick = lane == lax.rem(mine, per_block) * QUERY_HEADS + iota((QUERY_HEADS, LANES), 0)
    peak_of, sum_of = [], []
    for s in range(G):
        stat = stat_buf[s]
        peak_of.append(jnp.sum(jnp.where(pick, stat[0:1], 0.0), axis=1, keepdims=True))
        sum_of.append(jnp.sum(jnp.where(pick, stat[1:2], 0.0), axis=1, keepdims=True))
    peak_all = functools.reduce(jnp.maximum, peak_of)
    weighted = jnp.zeros((QUERY_HEADS, LANES), F32)
    sum_all = jnp.zeros((QUERY_HEADS, 1), F32)
    for s in range(G):
        factor = jnp.exp(peak_of[s] - peak_all)
        weighted += part_buf[s].astype(F32) * factor
        sum_all += sum_of[s] * factor
    attn = weighted / sum_all
    attn = jnp.concatenate(
        [attn[h * G : (h + 1) * G] for h in range(QUERY_HEADS // G)], axis=1
    ).astype(BF16)
    mixed = jnp.dot(attn, proj_v[...], preferred_element_type=F32)
    for c in range(WB):
        mix_f32[pl.ds(c, G, stride=WB), :] = mixed[:, c * LANES : (c + 1) * LANES]
    mix_send[...] = mix_f32[...].astype(BF16).reshape(G, WB, LANES)

    to_pack(lambda place, to: send(mix_send.at[place], mix_buf.at[mine], 3, to))
    mix_buf[mine] = mix_send[mine]
    res_row = residual[...].astype(F32)
    stream = jnp.concatenate(
        [res_row[:, c * LANES : (c + 1) * LANES] for c in range(WB)], axis=0
    )
    head_f32 = head[...].astype(F32)
    await_all(mix_buf, G - 1, recv_sem.at[3])
    stream += jnp.sum(mix_buf[...].astype(F32), axis=0)
    scale = lax.rsqrt(total(stream * stream) * (1.0 / width) + EPSILON)
    normed = (stream * scale * gain[...].astype(F32)).astype(BF16)
    norm_own[...] = normed

    to_all(lambda t, to: send(norm_own, norm_buf.at[me], 4, to))
    norm_buf[me] = norm_own[...]

    normed = normed.astype(F32)
    logits = jnp.zeros((E, LANES), F32)
    for c in range(WB):
        logits += router[:, c * LANES : (c + 1) * LANES].astype(F32) * normed[c : c + 1]
    logits = jnp.sum(logits, axis=1, keepdims=True)
    route_row = routes[pl.ds(sq, 1), :].astype(F32)
    topk = routes.shape[1]
    chosen = jnp.sum(
        jnp.where(iota((E, topk), 0).astype(F32) == route_row, 1.0, 0.0), axis=1, keepdims=True
    )
    masked = jnp.where(chosen > 0.5, logits, MASKED)
    power = jnp.where(
        chosen > 0.5, jnp.exp(masked - jnp.max(masked, axis=0, keepdims=True)), 0.0
    )
    gate_weight = power / jnp.sum(power, axis=0, keepdims=True)

    for load in loads[3:]:
        load.wait()
    await_all(norm_buf, N - 1, recv_sem.at[4])

    norm_f32[...] = norm_buf[...].astype(F32).reshape(N * WB, LANES)
    for c in range(WB):
        rows[:, c * LANES : (c + 1) * LANES] = norm_f32[pl.ds(c, N, stride=WB), :].astype(BF16)
    gate_act = jnp.dot(rows[...], gate_v[...], preferred_element_type=F32)
    up_act = jnp.dot(rows[...], up_v[...], preferred_element_type=F32)
    hidden = (gate_act / (1.0 + jnp.exp(-gate_act)) * up_act).astype(BF16)
    hidden_out[...] = hidden
    expert_out = jnp.dot(hidden, down_v[...], preferred_element_type=F32)
    for c in range(WB):
        out_f32[pl.ds(c, N, stride=WB), :] = expert_out[:, c * LANES : (c + 1) * LANES]
    out_send[...] = out_f32[...].astype(BF16).reshape(N, WB, LANES)

    slot = sq * E + dp * EN + ex
    to_all(lambda t, to: send(out_send.at[t], out_buf.at[slot], 5, to))
    out_buf[slot] = out_send[me]
    await_all(out_buf, N - 1, recv_sem.at[5])

    outs = out_buf[0:E].astype(F32)
    for half in range(1, SQ):
        outs += out_buf[half * E : (half + 1) * E].astype(F32)
    final = stream + jnp.sum(outs * gate_weight.reshape(E, 1, 1), axis=0)
    scale = lax.rsqrt(total(final * final) * (1.0 / width) + EPSILON)
    along = total(final * head_f32)
    reward = along * scale
    target = labels[...].astype(F32)
    decay = jnp.exp(-jnp.abs(reward))
    row_loss = jnp.maximum(reward, 0.0) + jnp.log1p(decay) - target * reward
    error = jnp.where(reward >= 0.0, 1.0, decay) / (1.0 + decay) - target
    d_mix = (
        (error * scale) * (head_f32 - final * (scale * scale * along * (1.0 / width)))
    ).astype(BF16).astype(F32)
    grad_send[...] = (gate_weight.reshape(E, 1, 1) * d_mix[None]).astype(BF16)

    to_all(
        lambda t, to: send(
            grad_send.at[to[0] * EN + to[2]], grad_buf.at[me], 6, to
        )
    )
    grad_buf[me] = grad_send[dp * EN + ex]
    route_dot = jnp.sum(jnp.sum(outs * d_mix[None], axis=1), axis=1, keepdims=True)
    mean_dot = jnp.sum(gate_weight * route_dot, axis=0, keepdims=True)
    d_logits = to_row(gate_weight * (route_dot - mean_dot), E)
    if E < LANES:
        d_logits = jnp.concatenate([d_logits, jnp.zeros((1, LANES - E), F32)], axis=1)
    dlog_own[...] = jnp.concatenate(
        [d_logits, jnp.broadcast_to(row_loss, (1, LANES))], axis=0
    )
    to_all(lambda t, to: send(dlog_own, dlog_buf.at[me], 7, to))
    dlog_buf[me] = dlog_own[...]

    await_all(grad_buf, N - 1, recv_sem.at[6])
    grad_f32[...] = grad_buf[...].astype(F32).reshape(N * WB, LANES)
    for c in range(WB):
        grads_out[:, c * LANES : (c + 1) * LANES] = grad_f32[
            pl.ds(c, N, stride=WB), :
        ].astype(BF16)

    share = width // N
    first = ((dp * SQ + sq) * EN + ex) * share
    own_columns = norm_f32[pl.ds(first // LANES, N, stride=WB), :]
    own_columns = pltpu.roll(own_columns, lax.rem(LANES - lax.rem(first, LANES), LANES), 1)
    await_all(dlog_buf, N - 1, recv_sem.at[7])
    loss_out[...] = jnp.sum(dlog_buf[:, 1, :], axis=0, keepdims=True)
    router_grad = lax.dot_general(
        dlog_buf[:, 0, :],
        own_columns,
        (((0,), (0,)), ((), ())),
        precision=lax.Precision.HIGHEST,
        preferred_element_type=F32,
    )
    router_out[...] = router_grad[0:E, 0:share].astype(BF16)

    for number, (buf, count) in enumerate(
        [
            (q_buf, G),
            (part_buf, G),
            (stat_buf, G),
            (mix_buf, G),
            (norm_buf, N),
            (out_buf, N),
            (grad_buf, N),
            (dlog_buf, N),
        ]
    ):
        await_all(buf, count - 1, send_sem.at[number])


def shards(
    sizes,
    keys,
    values,
    queries,
    residual,
    out_proj,
    norm_gain,
    router,
    w_gate,
    w_up,
    w_down,
    head_vec,
    routes,
    step_pos,
    labels,
    trace_len,
):
    DP, SQ, EN = sizes
    G, E = DP * SQ, DP * EN
    N = G * EN
    width = residual.shape[2]
    WB = width // LANES
    hidden_units = w_gate.shape[2]
    hbm = pl.BlockSpec(memory_space=pl.ANY)
    vmem = pl.BlockSpec(memory_space=pltpu.VMEM)
    message = (WB, LANES)
    loss, hidden, grads, grad_router = pl.pallas_call(
        functools.partial(kernel, sizes),
        out_shape=(
            jax.ShapeDtypeStruct((1, LANES), F32),
            jax.ShapeDtypeStruct((N, hidden_units), BF16),
            jax.ShapeDtypeStruct((N, width), BF16),
            jax.ShapeDtypeStruct((E, width // N), BF16),
        ),
        in_specs=[hbm, hbm, vmem, vmem, hbm, vmem, vmem, hbm, hbm, hbm, vmem, vmem, vmem, vmem, vmem],
        out_specs=(vmem, vmem, vmem, vmem),
        scratch_shapes=[
            pltpu.VMEM(keys.shape[1:], BF16),
            pltpu.VMEM(values.shape[1:], BF16),
            pltpu.VMEM(out_proj.shape, BF16),
            pltpu.VMEM(w_gate.shape[1:], BF16),
            pltpu.VMEM(w_up.shape[1:], BF16),
            pltpu.VMEM(w_down.shape[1:], BF16),
            pltpu.VMEM((QUERY_HEADS, LANES), BF16),
            pltpu.VMEM((G, QUERY_HEADS, LANES), BF16),
            pltpu.VMEM((G * QUERY_HEADS, LANES), F32),
            pltpu.VMEM((G, QUERY_HEADS, LANES), BF16),
            pltpu.VMEM((G, QUERY_HEADS, LANES), BF16),
            pltpu.VMEM((G * QUERY_HEADS // LANES, 8, LANES), F32),
            pltpu.VMEM((G, 8, LANES), F32),
            pltpu.VMEM((G * WB, LANES), F32),
            pltpu.VMEM((G,) + message, BF16),
            pltpu.VMEM((G,) + message, BF16),
            pltpu.VMEM(message, BF16),
            pltpu.VMEM((N,) + message, BF16),
            pltpu.VMEM((N * WB, LANES), F32),
            pltpu.VMEM((N, width), BF16),
            pltpu.VMEM((N * WB, LANES), F32),
            pltpu.VMEM((N,) + message, BF16),
            pltpu.VMEM((N,) + message, BF16),
            pltpu.VMEM((E,) + message, BF16),
            pltpu.VMEM((N,) + message, BF16),
            pltpu.VMEM((N * WB, LANES), F32),
            pltpu.VMEM((2, LANES), F32),
            pltpu.VMEM((N, 2, LANES), F32),
            pltpu.SemaphoreType.DMA((6,)),
            pltpu.SemaphoreType.DMA((8,)),
            pltpu.SemaphoreType.DMA((8,)),
        ],
        compiler_params=pltpu.CompilerParams(
            collective_id=0, has_side_effects=True, vmem_limit_bytes=56 * 1024 * 1024
        ),
    )(
        keys,
        values,
        queries[0],
        residual[0],
        out_proj,
        norm_gain.reshape(message),
        router.T,
        w_gate,
        w_up,
        w_down,
        head_vec.reshape(message),
        routes[0],
        step_pos,
        labels,
        trace_len,
    )
    grad_down = lax.dot_general(
        hidden, grads, (((0,), (0,)), ((), ())), preferred_element_type=F32
    ).astype(BF16)
    return loss[0, 0], grad_down[None], grad_router.T


def solution(mesh):
    sizes = (mesh.shape["dp"], mesh.shape["seq"], mesh.shape["expert"])
    return jax.shard_map(
        functools.partial(shards, sizes),
        mesh=mesh,
        in_specs=(
            P("expert", ("dp", "seq"), None),
            P("expert", ("dp", "seq"), None),
            P("expert", ("dp", "seq"), None),
            P("expert", ("dp", "seq"), None),
            P(("dp", "seq"), None),
            P(),
            P(),
            P(("dp", "expert"), None, "seq"),
            P(("dp", "expert"), None, "seq"),
            P(("dp", "expert"), "seq", None),
            P(),
            P("expert", "dp", None),
            P("expert", None),
            P("expert", ("dp", "seq")),
            P("expert", None),
        ),
        out_specs=(P(), P(("dp", "expert"), "seq", None), P(("dp", "seq", "expert"), None)),
        check_vma=False,
    )
```

```python
import functools

import jax
import jax.numpy as jnp
from jax import lax
from jax.experimental import pallas as pl
from jax.experimental.pallas import tpu as pltpu
from jax.sharding import PartitionSpec as P

QUERY_HEADS = 32
KEY_VALUE_HEADS = 4
HEAD_WIDTH = 128
LANES = 128
MASKED = -1e30
EPSILON = 1e-06
STAT_ROWS = 16
INPUTS = (
    "queries",
    "step_pos",
    "trace_len",
    "keys",
    "values",
    "residual",
    "norm_gain",
    "router",
    "head_vec",
    "routes",
    "labels",
    "out_proj",
    "w_gate",
    "w_up",
    "w_down",
)
MESH = pl.DeviceIdType.MESH
F32 = jnp.float32
BF16 = jnp.bfloat16


def iota(shape, axis):
    return lax.broadcasted_iota(jnp.int32, shape, axis)


def total(x):
    return jnp.sum(jnp.sum(x, axis=1, keepdims=True), axis=0, keepdims=True)


def to_row(column, n):
    eye = iota((n, n), 0) == iota((n, n), 1)
    return jnp.sum(jnp.where(eye, column, 0.0), axis=0, keepdims=True)


def to_column(row, n):
    eye = iota((n, n), 0) == iota((n, n), 1)
    return jnp.sum(jnp.where(eye, row, 0.0), axis=1, keepdims=True)


def split3(x):
    high = x.astype(BF16).astype(F32)
    rest = x - high
    middle = rest.astype(BF16).astype(F32)
    return [high, middle, rest - middle]


def kernel(sizes, names, *refs):
    r = dict(zip(names, refs))
    DP, SQ, EN = sizes
    G, E = DP * SQ, DP * EN
    N = G * EN
    unroll = N <= 32
    proj_v, gate_v, up_v, down_v = r["out_proj"], r["w_gate"], r["w_up"], r["w_down"]
    width = proj_v.shape[1]
    WB = width // LANES
    dp, sq, ex = lax.axis_index("dp"), lax.axis_index("seq"), lax.axis_index("expert")
    mine = dp * SQ + sq
    expert = dp * EN + ex
    me = sq * E + expert
    tokens = r["keys"].shape[0]
    load_sem, send_sem, recv_sem = r["load_sem"], r["send_sem"], r["recv_sem"]

    loads = {}
    for i, name in enumerate(INPUTS):
        source, target = r["in_" + name], r[name]
        if len(source.shape) > len(target.shape):
            source = source.at[0]
        loads[name] = pltpu.make_async_copy(source, target, load_sem.at[i])
        loads[name].start()

    if unroll:
        near_dp = [lax.rem(dp + a, DP) for a in range(DP)]
        near_sq = [lax.rem(sq + a, SQ) for a in range(SQ)]
        near_ex = [lax.rem(ex + a, EN) for a in range(EN)]

        def near(a, b, c):
            return near_dp[a], near_sq[b], near_ex[c]
    else:

        def near(a, b, c):
            return lax.rem(dp + a, DP), lax.rem(sq + b, SQ), lax.rem(ex + c, EN)

    def each(first, last, body):
        if unroll:
            for i in range(first, last):
                body(i)
        else:

            def step(i, carry):
                body(i)
                return carry

            lax.fori_loop(first, last, step, 0)

    def to_pack(body):
        each(1, G, lambda i: body(near(i // SQ, i % SQ, 0)))

    def to_plane(body):
        each(1, E, lambda i: body(near(i // EN, 0, i % EN)))

    def to_pair(body):
        each(1, SQ, lambda i: body(near(0, i, 0)))

    barrier = pltpu.get_barrier_semaphore()

    def greet(to):
        pl.semaphore_signal(barrier, inc=1, device_id=to, device_id_type=MESH)

    to_pack(greet)
    each(1, EN, lambda c: each(0, DP, lambda a: greet(near(a, 0, c))))
    partners = G - 1 + (EN - 1) * DP

    def send(source, target, number, to):
        pltpu.make_async_remote_copy(
            src_ref=source,
            dst_ref=target,
            send_sem=send_sem.at[number],
            recv_sem=recv_sem.at[number],
            device_id=to,
            device_id_type=MESH,
        ).start()

    def await_all(buf, count, sem):
        span = buf.at[pl.ds(0, count)]
        pltpu.make_async_copy(span, span, sem).wait()

    q_own, q_buf, q_f32 = r["q_own"], r["q_buf"], r["q_f32"]
    loads["queries"].wait()
    q_row = r["queries"][...].astype(F32)
    q_own[...] = jnp.concatenate(
        [q_row[:, h * LANES : (h + 1) * LANES] for h in range(QUERY_HEADS)], axis=0
    ).astype(BF16)
    pl.semaphore_wait(barrier, partners)

    to_pack(lambda to: send(q_own, q_buf.at[mine], 0, to))
    q_buf[mine] = q_own[...]

    for name in INPUTS:
        if name not in ("queries", "out_proj", "w_gate", "w_up", "w_down"):
            loads[name].wait()
    traces = r["trace_len"].shape[1]
    pos_col = to_column(r["step_pos"][...].astype(F32), G)
    len_row = r["trace_len"][...].astype(F32)
    len_col = to_column(len_row, traces)
    before = iota((traces, traces), 0) <= iota((traces, traces), 1)
    ends_row = jnp.sum(jnp.where(before, len_col, 0.0), axis=0, keepdims=True)
    start_col = jnp.sum(jnp.where(ends_row <= pos_col, len_row, 0.0), axis=1, keepdims=True)
    key_pos = (mine * tokens + iota((G, tokens), 1)).astype(F32)
    allowed = jnp.where((key_pos <= pos_col) & (key_pos >= start_col), 1.0, 0.0)
    group = QUERY_HEADS // KEY_VALUE_HEADS
    allowed = jnp.concatenate([allowed] * group, axis=0) > 0.5
    await_all(q_buf, G - 1, recv_sem.at[0])

    part_send, part_buf = r["part_send"], r["part_buf"]
    key_v, value_v = r["keys"], r["values"]
    q_f32[...] = q_buf[...].astype(F32).reshape(G * QUERY_HEADS, LANES)
    peaks, sums = [], []
    owners = G // KEY_VALUE_HEADS
    for g in range(KEY_VALUE_HEADS):
        q_part = jnp.concatenate(
            [q_f32[pl.ds(g * group + h, G, stride=QUERY_HEADS), :] for h in range(group)], axis=0
        ).astype(BF16)
        columns = slice(g * HEAD_WIDTH, (g + 1) * HEAD_WIDTH)
        score = (
            lax.dot_general(
                q_part, key_v[:, columns], (((1,), (1,)), ((), ())), preferred_element_type=F32
            )
            * HEAD_WIDTH ** (-0.5)
        )
        score = jnp.where(allowed, score, MASKED)
        peak = jnp.max(score, axis=1, keepdims=True)
        weight = jnp.where(allowed, jnp.exp(score - peak), 0.0)
        peaks.append(peak)
        sums.append(jnp.sum(weight, axis=1, keepdims=True))
        part = jnp.dot(weight.astype(BF16), value_v[:, columns], preferred_element_type=F32)
        part_send[g * owners : (g + 1) * owners, 0:QUERY_HEADS] = part.astype(BF16).reshape(
            owners, QUERY_HEADS, LANES
        )
    peaks, sums = jnp.concatenate(peaks, axis=0), jnp.concatenate(sums, axis=0)
    per_block = LANES // QUERY_HEADS
    for b in range(G // per_block):
        span = slice(b * LANES, (b + 1) * LANES)
        stat = jnp.concatenate(
            split3(to_row(peaks[span], LANES))
            + split3(to_row(sums[span], LANES))
            + [jnp.zeros((STAT_ROWS - 6, LANES), F32)],
            axis=0,
        ).astype(BF16)
        part_send[b * per_block : (b + 1) * per_block, QUERY_HEADS:] = jnp.broadcast_to(
            stat[None], (per_block, STAT_ROWS, LANES)
        )

    to_pack(lambda to: send(part_send.at[to[0] * SQ + to[1]], part_buf.at[mine], 1, to))
    part_buf[mine] = part_send[mine]
    loads["out_proj"].wait()
    lane = iota((QUERY_HEADS, LANES), 1)
    pick = lane == lax.rem(mine, per_block) * QUERY_HEADS + iota((QUERY_HEADS, LANES), 0)
    await_all(part_buf, G - 1, recv_sem.at[1])

    peak_of, sum_of = [], []
    for s in range(G):
        stat = part_buf[s, QUERY_HEADS:].astype(F32)
        peak_row = stat[0:1] + stat[1:2] + stat[2:3]
        sum_row = stat[3:4] + stat[4:5] + stat[5:6]
        peak_of.append(jnp.sum(jnp.where(pick, peak_row, 0.0), axis=1, keepdims=True))
        sum_of.append(jnp.sum(jnp.where(pick, sum_row, 0.0), axis=1, keepdims=True))
    peak_all = functools.reduce(jnp.maximum, peak_of)
    weighted = jnp.zeros((QUERY_HEADS, LANES), F32)
    sum_all = jnp.zeros((QUERY_HEADS, 1), F32)
    for s in range(G):
        factor = jnp.exp(peak_of[s] - peak_all)
        weighted += part_buf[s, 0:QUERY_HEADS].astype(F32) * factor
        sum_all += sum_of[s] * factor
    attn = weighted / sum_all
    attn = jnp.concatenate(
        [attn[h * G : (h + 1) * G] for h in range(QUERY_HEADS // G)], axis=1
    ).astype(BF16)
    mixed = jnp.dot(attn, proj_v[...], preferred_element_type=F32)
    mix_f32, mix_send, mix_buf = r["mix_f32"], r["mix_send"], r["mix_buf"]
    for c in range(WB):
        mix_f32[pl.ds(c, G, stride=WB), :] = mixed[:, c * LANES : (c + 1) * LANES]
    mix_send[...] = mix_f32[...].astype(BF16).reshape(G, WB, LANES)

    to_pack(lambda to: send(mix_send.at[to[0] * SQ + to[1]], mix_buf.at[mine], 2, to))
    mix_buf[mine] = mix_send[mine]
    res_row = r["residual"][...].astype(F32)
    stream = jnp.concatenate(
        [res_row[:, c * LANES : (c + 1) * LANES] for c in range(WB)], axis=0
    )
    head_f32 = r["head_vec"][...].astype(F32)
    gain = r["norm_gain"][...].astype(F32)
    await_all(mix_buf, G - 1, recv_sem.at[2])
    stream += jnp.sum(mix_buf[...].astype(F32), axis=0)
    scale = lax.rsqrt(total(stream * stream) * (1.0 / width) + EPSILON)
    normed = (stream * scale * gain).astype(BF16)
    norm_own, norm_buf, norm_f32, rows = r["norm_own"], r["norm_buf"], r["norm_f32"], r["rows"]
    norm_own[...] = normed

    to_plane(lambda to: send(norm_own, norm_buf.at[me], 3, to))
    norm_buf[me] = norm_own[...]
    plane = pl.ds(sq * E, E)

    normed = normed.astype(F32)
    logits = jnp.zeros((E, LANES), F32)
    for c in range(WB):
        logits += r["router"][:, c * LANES : (c + 1) * LANES].astype(F32) * normed[c : c + 1]
    logits = jnp.sum(logits, axis=1, keepdims=True)
    route_row = r["routes"][pl.ds(sq, 1), :].astype(F32)
    topk = r["routes"].shape[1]
    chosen = jnp.sum(
        jnp.where(iota((E, topk), 0).astype(F32) == route_row, 1.0, 0.0), axis=1, keepdims=True
    )
    masked = jnp.where(chosen > 0.5, logits, MASKED)
    power = jnp.where(
        chosen > 0.5, jnp.exp(masked - jnp.max(masked, axis=0, keepdims=True)), 0.0
    )
    gate_weight = power / jnp.sum(power, axis=0, keepdims=True)

    await_all(norm_buf, E - 1, recv_sem.at[3])
    to_pair(lambda to: send(norm_buf.at[plane], norm_buf.at[plane], 4, to))
    for name in ("w_gate", "w_up", "w_down"):
        loads[name].wait()
    await_all(norm_buf, N - E, recv_sem.at[4])

    norm_f32[...] = norm_buf[...].astype(F32).reshape(N * WB, LANES)
    for c in range(WB):
        rows[:, c * LANES : (c + 1) * LANES] = norm_f32[pl.ds(c, N, stride=WB), :].astype(BF16)
    gate_act = jnp.dot(rows[...], gate_v[...], preferred_element_type=F32)
    up_act = jnp.dot(rows[...], up_v[...], preferred_element_type=F32)
    hidden = (gate_act / (1.0 + jnp.exp(-gate_act)) * up_act).astype(BF16)
    r["hidden"][...] = hidden
    stores = [pltpu.make_async_copy(r["hidden"], r["out_hidden"], load_sem.at[0])]
    stores[0].start()
    expert_out = jnp.dot(hidden, down_v[...], preferred_element_type=F32)
    out_f32, half_send, half_buf = r["out_f32"], r["half_send"], r["half_buf"]
    out_send, out_buf = r["out_send"], r["out_buf"]
    for c in range(WB):
        out_f32[pl.ds(c, N, stride=WB), :] = expert_out[:, c * LANES : (c + 1) * LANES]
    half_send[...] = out_f32[...].astype(BF16).reshape(SQ, E, WB, LANES)

    to_pair(lambda to: send(half_send.at[to[1]], half_buf.at[sq], 5, to))
    await_all(half_buf, SQ - 1, recv_sem.at[5])
    outs = out_f32[pl.ds(pl.multiple_of(sq * (E * WB), E * WB), E * WB), :].reshape(E, WB, LANES)
    for i in range(1, SQ):
        outs += half_buf[lax.rem(sq + i, SQ)].astype(F32)
    out_send[...] = outs.astype(BF16)
    to_plane(lambda to: send(out_send.at[to[0] * EN + to[2]], out_buf.at[expert], 6, to))
    out_buf[expert] = out_send[expert]
    own_label = r["labels"][...].astype(F32)
    weight_column = gate_weight.reshape(E, 1, 1)
    await_all(out_buf, E - 1, recv_sem.at[6])

    outs = out_buf[...].astype(F32)
    final = stream + jnp.sum(outs * weight_column, axis=0)
    scale = lax.rsqrt(total(final * final) * (1.0 / width) + EPSILON)
    along = total(final * head_f32)
    reward = along * scale
    decay = jnp.exp(-jnp.abs(reward))
    row_loss = jnp.maximum(reward, 0.0) + jnp.log1p(decay) - own_label * reward
    error = jnp.where(reward >= 0.0, 1.0, decay) / (1.0 + decay) - own_label
    d_mix = (
        (error * scale) * (head_f32 - final * (scale * scale * along * (1.0 / width)))
    ).astype(BF16).astype(F32)
    grad_send, grad_buf, grad_f32 = r["grad_send"], r["grad_buf"], r["grad_f32"]
    dlog_own, dlog_buf = r["dlog_own"], r["dlog_buf"]
    grad_send[...] = (weight_column * d_mix[None]).astype(BF16)

    to_plane(lambda to: send(grad_send.at[to[0] * EN + to[2]], grad_buf.at[me], 7, to))
    grad_buf[me] = grad_send[expert]
    route_dot = jnp.sum(jnp.sum(outs * d_mix[None], axis=1), axis=1, keepdims=True)
    mean_dot = jnp.sum(gate_weight * route_dot, axis=0, keepdims=True)
    d_logits = to_row(gate_weight * (route_dot - mean_dot), E)
    if E < LANES:
        d_logits = jnp.concatenate([d_logits, jnp.zeros((1, LANES - E), F32)], axis=1)
    dlog_own[...] = jnp.concatenate(
        [d_logits, jnp.broadcast_to(row_loss, (1, LANES))], axis=0
    )
    to_plane(lambda to: send(dlog_own, dlog_buf.at[me], 9, to))
    dlog_buf[me] = dlog_own[...]
    share = width // N
    first = (mine * EN + ex) * share
    own_columns = norm_f32[pl.ds(first // LANES, N, stride=WB), :]
    own_columns = pltpu.roll(own_columns, lax.rem(LANES - lax.rem(first, LANES), LANES), 1)

    await_all(grad_buf, E - 1, recv_sem.at[7])
    to_pair(lambda to: send(grad_buf.at[plane], grad_buf.at[plane], 8, to))
    await_all(dlog_buf, E - 1, recv_sem.at[9])
    to_pair(lambda to: send(dlog_buf.at[plane], dlog_buf.at[plane], 10, to))
    await_all(grad_buf, N - E, recv_sem.at[8])
    grad_f32[...] = grad_buf[...].astype(F32).reshape(N * WB, LANES)
    for c in range(WB):
        r["grads"][:, c * LANES : (c + 1) * LANES] = grad_f32[
            pl.ds(c, N, stride=WB), :
        ].astype(BF16)
    stores.append(pltpu.make_async_copy(r["grads"], r["out_grads"], load_sem.at[1]))
    stores[-1].start()
    await_all(dlog_buf, N - E, recv_sem.at[10])
    r["loss"][...] = jnp.sum(dlog_buf[:, 1, :], axis=0, keepdims=True)
    router_grad = lax.dot_general(
        dlog_buf[:, 0, :],
        own_columns,
        (((0,), (0,)), ((), ())),
        precision=lax.Precision.HIGHEST,
        preferred_element_type=F32,
    )
    r["router_grad"][...] = router_grad[0:E, 0:share].astype(BF16)
    stores.append(pltpu.make_async_copy(r["loss"], r["out_loss"], load_sem.at[2]))
    stores[-1].start()
    stores.append(pltpu.make_async_copy(r["router_grad"], r["out_router"], load_sem.at[3]))
    stores[-1].start()

    for number, (buf, count) in enumerate(
        [
            (q_buf, G - 1),
            (part_buf, G - 1),
            (mix_buf, G - 1),
            (norm_buf, E - 1),
            (norm_buf, N - E),
            (half_buf, SQ - 1),
            (out_buf, E - 1),
            (grad_buf, E - 1),
            (grad_buf, N - E),
            (dlog_buf, E - 1),
            (dlog_buf, N - E),
        ]
    ):
        await_all(buf, count, send_sem.at[number])
    for store in stores:
        store.wait()


def down_kernel(*refs):
    sources, (loss_out, down_out, router_out), targets = refs[:4], refs[4:7], refs[7:11]
    stage, sem = refs[11:]
    loads = [
        pltpu.make_async_copy(source, target, sem.at[i])
        for i, (source, target) in enumerate(zip(sources, targets))
    ]
    for load in loads:
        load.start()
    for load in loads:
        load.wait()
    hidden, grads, loss, router_grad = targets
    step = stage.shape[1] // 4
    stores = []
    for i in range(4):
        columns = pl.ds(i * step, step)
        stage[:, i * step : (i + 1) * step] = lax.dot_general(
            hidden[...],
            grads[:, i * step : (i + 1) * step],
            (((0,), (0,)), ((), ())),
            preferred_element_type=F32,
        ).astype(BF16)
        stores.append(
            pltpu.make_async_copy(stage.at[:, columns], down_out.at[0, :, columns], sem.at[i])
        )
        stores[-1].start()
    loss_out[...] = loss[:, 0:1]
    router_out[...] = router_grad[...]
    for store in stores:
        store.wait()


def shards(
    sizes,
    keys,
    values,
    queries,
    residual,
    out_proj,
    norm_gain,
    router,
    w_gate,
    w_up,
    w_down,
    head_vec,
    routes,
    step_pos,
    labels,
    trace_len,
):
    DP, SQ, EN = sizes
    G, E = DP * SQ, DP * EN
    N = G * EN
    width = residual.shape[2]
    WB = width // LANES
    hidden_units = w_gate.shape[2]
    hbm = pl.BlockSpec(memory_space=pl.ANY)
    vmem = pl.BlockSpec(memory_space=pltpu.VMEM)
    message = (WB, LANES)
    operands = dict(
        queries=queries[0],
        step_pos=step_pos,
        trace_len=trace_len,
        keys=keys,
        values=values,
        residual=residual[0],
        norm_gain=norm_gain.reshape(message),
        router=router.T,
        head_vec=head_vec.reshape(message),
        routes=routes[0],
        labels=labels,
        out_proj=out_proj,
        w_gate=w_gate,
        w_up=w_up,
        w_down=w_down,
    )
    outs = dict(
        out_loss=jax.ShapeDtypeStruct((1, LANES), F32),
        out_hidden=jax.ShapeDtypeStruct((N, hidden_units), BF16),
        out_grads=jax.ShapeDtypeStruct((N, width), BF16),
        out_router=jax.ShapeDtypeStruct((E, width // N), BF16),
    )
    scratch = {
        name: pltpu.VMEM(operands[name].shape[-2:], operands[name].dtype) for name in INPUTS
    }
    scratch.update(
        loss=pltpu.VMEM((1, LANES), F32),
        hidden=pltpu.VMEM((N, hidden_units), BF16),
        grads=pltpu.VMEM((N, width), BF16),
        router_grad=pltpu.VMEM((E, width // N), BF16),
        q_own=pltpu.VMEM((QUERY_HEADS, LANES), BF16),
        q_buf=pltpu.VMEM((G, QUERY_HEADS, LANES), BF16),
        q_f32=pltpu.VMEM((G * QUERY_HEADS, LANES), F32),
        part_send=pltpu.VMEM((G, QUERY_HEADS + STAT_ROWS, LANES), BF16),
        part_buf=pltpu.VMEM((G, QUERY_HEADS + STAT_ROWS, LANES), BF16),
        mix_f32=pltpu.VMEM((G * WB, LANES), F32),
        mix_send=pltpu.VMEM((G,) + message, BF16),
        mix_buf=pltpu.VMEM((G,) + message, BF16),
        norm_own=pltpu.VMEM(message, BF16),
        norm_buf=pltpu.VMEM((N,) + message, BF16),
        norm_f32=pltpu.VMEM((N * WB, LANES), F32),
        rows=pltpu.VMEM((N, width), BF16),
        out_f32=pltpu.VMEM((N * WB, LANES), F32),
        half_send=pltpu.VMEM((SQ, E) + message, BF16),
        half_buf=pltpu.VMEM((SQ, E) + message, BF16),
        out_send=pltpu.VMEM((E,) + message, BF16),
        out_buf=pltpu.VMEM((E,) + message, BF16),
        grad_send=pltpu.VMEM((E,) + message, BF16),
        grad_buf=pltpu.VMEM((N,) + message, BF16),
        grad_f32=pltpu.VMEM((N * WB, LANES), F32),
        dlog_own=pltpu.VMEM((2, LANES), F32),
        dlog_buf=pltpu.VMEM((N, 2, LANES), F32),
        load_sem=pltpu.SemaphoreType.DMA((len(INPUTS),)),
        send_sem=pltpu.SemaphoreType.DMA((11,)),
        recv_sem=pltpu.SemaphoreType.DMA((11,)),
    )
    names = ["in_" + name for name in INPUTS] + list(outs) + list(scratch)
    loss, hidden, grads, grad_router = pl.pallas_call(
        functools.partial(kernel, sizes, names),
        out_shape=tuple(outs.values()),
        in_specs=[hbm] * len(INPUTS),
        out_specs=(hbm,) * len(outs),
        scratch_shapes=list(scratch.values()),
        compiler_params=pltpu.CompilerParams(
            collective_id=0, has_side_effects=True, vmem_limit_bytes=56 * 1024 * 1024
        ),
    )(*[operands[name] for name in INPUTS])
    loss, grad_down, grad_router = pl.pallas_call(
        down_kernel,
        out_shape=(
            jax.ShapeDtypeStruct((1, 1), F32),
            jax.ShapeDtypeStruct((1, hidden_units, width), BF16),
            jax.ShapeDtypeStruct((E, width // N), BF16),
        ),
        in_specs=[hbm] * 4,
        out_specs=(vmem, hbm, vmem),
        scratch_shapes=[
            pltpu.VMEM((N, hidden_units), BF16),
            pltpu.VMEM((N, width), BF16),
            pltpu.VMEM((1, LANES), F32),
            pltpu.VMEM((E, width // N), BF16),
            pltpu.VMEM((hidden_units, width), BF16),
            pltpu.SemaphoreType.DMA((4,)),
        ],
        compiler_params=pltpu.CompilerParams(vmem_limit_bytes=32 * 1024 * 1024),
    )(hidden, grads, loss, grad_router)
    return loss.reshape(()), grad_down, grad_router.T


def solution(mesh):
    sizes = (mesh.shape["dp"], mesh.shape["seq"], mesh.shape["expert"])
    return jax.shard_map(
        functools.partial(shards, sizes),
        mesh=mesh,
        in_specs=(
            P("expert", ("dp", "seq"), None),
            P("expert", ("dp", "seq"), None),
            P("expert", ("dp", "seq"), None),
            P("expert", ("dp", "seq"), None),
            P(("dp", "seq"), None),
            P(),
            P(),
            P(("dp", "expert"), None, "seq"),
            P(("dp", "expert"), None, "seq"),
            P(("dp", "expert"), "seq", None),
            P(),
            P("expert", "dp", None),
            P("expert", None),
            P("expert", ("dp", "seq")),
            P("expert", None),
        ),
        out_specs=(P(), P(("dp", "expert"), "seq", None), P(("dp", "seq", "expert"), None)),
        check_vma=False,
    )
```

```python
import functools

import jax
import jax.numpy as jnp
from jax import lax
from jax.experimental import pallas as pl
from jax.experimental.pallas import tpu as pltpu
from jax.sharding import PartitionSpec as P

QUERY_HEADS = 32
KEY_VALUE_HEADS = 4
HEAD_WIDTH = 128
LANES = 128
MASKED = -1e30
EPSILON = 1e-06
STAT_ROWS = 16
INPUTS = (
    "queries",
    "step_pos",
    "trace_len",
    "keys",
    "values",
    "residual",
    "norm_gain",
    "router",
    "head_vec",
    "routes",
    "labels",
    "out_proj",
    "w_gate",
    "w_up",
    "w_down",
)
MESH = pl.DeviceIdType.MESH
F32 = jnp.float32
BF16 = jnp.bfloat16


def iota(shape, axis):
    return lax.broadcasted_iota(jnp.int32, shape, axis)


def total(x):
    return jnp.sum(jnp.sum(x, axis=1, keepdims=True), axis=0, keepdims=True)


def to_row(column, n):
    eye = iota((n, n), 0) == iota((n, n), 1)
    return jnp.sum(jnp.where(eye, column, 0.0), axis=0, keepdims=True)


def to_column(row, n):
    eye = iota((n, n), 0) == iota((n, n), 1)
    return jnp.sum(jnp.where(eye, row, 0.0), axis=1, keepdims=True)


def split3(x):
    high = x.astype(BF16).astype(F32)
    rest = x - high
    middle = rest.astype(BF16).astype(F32)
    return [high, middle, rest - middle]


def kernel(sizes, names, *refs):
    r = dict(zip(names, refs))
    DP, SQ, EN = sizes
    G, E = DP * SQ, DP * EN
    N = G * EN
    unroll = N <= 32
    proj_v, gate_v, up_v, down_v = r["out_proj"], r["w_gate"], r["w_up"], r["w_down"]
    width = proj_v.shape[1]
    WB = width // LANES
    dp, sq, ex = lax.axis_index("dp"), lax.axis_index("seq"), lax.axis_index("expert")
    mine = dp * SQ + sq
    expert = dp * EN + ex
    me = sq * E + expert
    tokens = r["keys"].shape[0]
    load_sem, send_sem, recv_sem = r["load_sem"], r["send_sem"], r["recv_sem"]

    loads = {}
    for i, name in enumerate(INPUTS):
        source, target = r["in_" + name], r[name]
        if len(source.shape) > len(target.shape):
            source = source.at[0]
        loads[name] = pltpu.make_async_copy(source, target, load_sem.at[i])
        loads[name].start()

    if unroll:
        near_dp = [lax.rem(dp + a, DP) for a in range(DP)]
        near_sq = [lax.rem(sq + a, SQ) for a in range(SQ)]
        near_ex = [lax.rem(ex + a, EN) for a in range(EN)]

        def near(a, b, c):
            return near_dp[a], near_sq[b], near_ex[c]
    else:

        def near(a, b, c):
            return lax.rem(dp + a, DP), lax.rem(sq + b, SQ), lax.rem(ex + c, EN)

    def each(first, last, body):
        if unroll:
            for i in range(first, last):
                body(i)
        else:

            def step(i, carry):
                body(i)
                return carry

            lax.fori_loop(first, last, step, 0)

    def to_pack(body):
        each(1, G, lambda i: body(near(i // SQ, i % SQ, 0)))

    def to_all(body):
        each(1, N, lambda i: body(near(i // (SQ * EN), (i // EN) % SQ, i % EN)))

    barrier = pltpu.get_barrier_semaphore()

    def greet(to):
        pl.semaphore_signal(barrier, inc=1, device_id=to, device_id_type=MESH)

    to_all(greet)

    def send(source, target, number, to):
        pltpu.make_async_remote_copy(
            src_ref=source,
            dst_ref=target,
            send_sem=send_sem.at[number],
            recv_sem=recv_sem.at[number],
            device_id=to,
            device_id_type=MESH,
        ).start()

    def await_all(buf, count, sem):
        span = buf.at[pl.ds(0, count)]
        pltpu.make_async_copy(span, span, sem).wait()

    q_own, q_buf, q_f32 = r["q_own"], r["q_buf"], r["q_f32"]
    loads["queries"].wait()
    q_row = r["queries"][...].astype(F32)
    q_own[...] = jnp.concatenate(
        [q_row[:, h * LANES : (h + 1) * LANES] for h in range(QUERY_HEADS)], axis=0
    ).astype(BF16)
    pl.semaphore_wait(barrier, N - 1)

    to_pack(lambda to: send(q_own, q_buf.at[mine], 0, to))
    q_buf[mine] = q_own[...]

    for name in INPUTS:
        if name not in ("queries", "out_proj", "w_gate", "w_up", "w_down"):
            loads[name].wait()
    traces = r["trace_len"].shape[1]
    pos_col = to_column(r["step_pos"][...].astype(F32), G)
    len_row = r["trace_len"][...].astype(F32)
    len_col = to_column(len_row, traces)
    before = iota((traces, traces), 0) <= iota((traces, traces), 1)
    ends_row = jnp.sum(jnp.where(before, len_col, 0.0), axis=0, keepdims=True)
    start_col = jnp.sum(jnp.where(ends_row <= pos_col, len_row, 0.0), axis=1, keepdims=True)
    key_pos = (mine * tokens + iota((G, tokens), 1)).astype(F32)
    allowed = jnp.where((key_pos <= pos_col) & (key_pos >= start_col), 1.0, 0.0)
    group = QUERY_HEADS // KEY_VALUE_HEADS
    allowed = jnp.concatenate([allowed] * group, axis=0) > 0.5
    await_all(q_buf, G - 1, recv_sem.at[0])

    part_send, part_buf = r["part_send"], r["part_buf"]
    key_v, value_v = r["keys"], r["values"]
    q_f32[...] = q_buf[...].astype(F32).reshape(G * QUERY_HEADS, LANES)
    peaks, sums = [], []
    owners = G // KEY_VALUE_HEADS
    for g in range(KEY_VALUE_HEADS):
        q_part = jnp.concatenate(
            [q_f32[pl.ds(g * group + h, G, stride=QUERY_HEADS), :] for h in range(group)], axis=0
        ).astype(BF16)
        columns = slice(g * HEAD_WIDTH, (g + 1) * HEAD_WIDTH)
        score = (
            lax.dot_general(
                q_part, key_v[:, columns], (((1,), (1,)), ((), ())), preferred_element_type=F32
            )
            * HEAD_WIDTH ** (-0.5)
        )
        score = jnp.where(allowed, score, MASKED)
        peak = jnp.max(score, axis=1, keepdims=True)
        weight = jnp.where(allowed, jnp.exp(score - peak), 0.0)
        peaks.append(peak)
        sums.append(jnp.sum(weight, axis=1, keepdims=True))
        part = jnp.dot(weight.astype(BF16), value_v[:, columns], preferred_element_type=F32)
        part_send[g * owners : (g + 1) * owners, 0:QUERY_HEADS] = part.astype(BF16).reshape(
            owners, QUERY_HEADS, LANES
        )
    peaks, sums = jnp.concatenate(peaks, axis=0), jnp.concatenate(sums, axis=0)
    per_block = LANES // QUERY_HEADS
    for b in range(G // per_block):
        span = slice(b * LANES, (b + 1) * LANES)
        stat = jnp.concatenate(
            split3(to_row(peaks[span], LANES))
            + split3(to_row(sums[span], LANES))
            + [jnp.zeros((STAT_ROWS - 6, LANES), F32)],
            axis=0,
        ).astype(BF16)
        part_send[b * per_block : (b + 1) * per_block, QUERY_HEADS:] = jnp.broadcast_to(
            stat[None], (per_block, STAT_ROWS, LANES)
        )

    to_pack(lambda to: send(part_send.at[to[0] * SQ + to[1]], part_buf.at[mine], 1, to))
    part_buf[mine] = part_send[mine]
    loads["out_proj"].wait()
    lane = iota((QUERY_HEADS, LANES), 1)
    pick = lane == lax.rem(mine, per_block) * QUERY_HEADS + iota((QUERY_HEADS, LANES), 0)
    await_all(part_buf, G - 1, recv_sem.at[1])

    peak_of, sum_of = [], []
    for s in range(G):
        stat = part_buf[s, QUERY_HEADS:].astype(F32)
        peak_row = stat[0:1] + stat[1:2] + stat[2:3]
        sum_row = stat[3:4] + stat[4:5] + stat[5:6]
        peak_of.append(jnp.sum(jnp.where(pick, peak_row, 0.0), axis=1, keepdims=True))
        sum_of.append(jnp.sum(jnp.where(pick, sum_row, 0.0), axis=1, keepdims=True))
    peak_all = functools.reduce(jnp.maximum, peak_of)
    weighted = jnp.zeros((QUERY_HEADS, LANES), F32)
    sum_all = jnp.zeros((QUERY_HEADS, 1), F32)
    for s in range(G):
        factor = jnp.exp(peak_of[s] - peak_all)
        weighted += part_buf[s, 0:QUERY_HEADS].astype(F32) * factor
        sum_all += sum_of[s] * factor
    attn = weighted / sum_all
    attn = jnp.concatenate(
        [attn[h * G : (h + 1) * G] for h in range(QUERY_HEADS // G)], axis=1
    ).astype(BF16)
    mixed = jnp.dot(attn, proj_v[...], preferred_element_type=F32)
    mix_f32, mix_send, mix_buf = r["mix_f32"], r["mix_send"], r["mix_buf"]
    for c in range(WB):
        mix_f32[pl.ds(c, G, stride=WB), :] = mixed[:, c * LANES : (c + 1) * LANES]
    mix_send[...] = mix_f32[...].astype(BF16).reshape(G, WB, LANES)

    to_pack(lambda to: send(mix_send.at[to[0] * SQ + to[1]], mix_buf.at[mine], 2, to))
    mix_buf[mine] = mix_send[mine]
    res_row = r["residual"][...].astype(F32)
    stream = jnp.concatenate(
        [res_row[:, c * LANES : (c + 1) * LANES] for c in range(WB)], axis=0
    )
    head_f32 = r["head_vec"][...].astype(F32)
    gain = r["norm_gain"][...].astype(F32)
    await_all(mix_buf, G - 1, recv_sem.at[2])
    stream += jnp.sum(mix_buf[...].astype(F32), axis=0)
    scale = lax.rsqrt(total(stream * stream) * (1.0 / width) + EPSILON)
    normed = (stream * scale * gain).astype(BF16)
    norm_own, norm_buf, norm_f32, rows = r["norm_own"], r["norm_buf"], r["norm_f32"], r["rows"]
    norm_own[...] = normed

    to_all(lambda to: send(norm_own, norm_buf.at[me], 3, to))
    norm_buf[me] = norm_own[...]

    normed = normed.astype(F32)
    logits = jnp.zeros((E, LANES), F32)
    for c in range(WB):
        logits += r["router"][:, c * LANES : (c + 1) * LANES].astype(F32) * normed[c : c + 1]
    logits = jnp.sum(logits, axis=1, keepdims=True)
    route_row = r["routes"][pl.ds(sq, 1), :].astype(F32)
    topk = r["routes"].shape[1]
    chosen = jnp.sum(
        jnp.where(iota((E, topk), 0).astype(F32) == route_row, 1.0, 0.0), axis=1, keepdims=True
    )
    masked = jnp.where(chosen > 0.5, logits, MASKED)
    power = jnp.where(
        chosen > 0.5, jnp.exp(masked - jnp.max(masked, axis=0, keepdims=True)), 0.0
    )
    gate_weight = power / jnp.sum(power, axis=0, keepdims=True)

    for name in ("w_gate", "w_up", "w_down"):
        loads[name].wait()
    await_all(norm_buf, N - 1, recv_sem.at[3])

    norm_f32[...] = norm_buf[...].astype(F32).reshape(N * WB, LANES)
    for c in range(WB):
        rows[:, c * LANES : (c + 1) * LANES] = norm_f32[pl.ds(c, N, stride=WB), :].astype(BF16)
    gate_act = jnp.dot(rows[...], gate_v[...], preferred_element_type=F32)
    up_act = jnp.dot(rows[...], up_v[...], preferred_element_type=F32)
    hidden = (gate_act / (1.0 + jnp.exp(-gate_act)) * up_act).astype(BF16)
    r["hidden"][...] = hidden
    stores = [pltpu.make_async_copy(r["hidden"], r["out_hidden"], load_sem.at[0])]
    stores[0].start()
    expert_out = jnp.dot(hidden, down_v[...], preferred_element_type=F32)
    out_f32, out_send, out_buf = r["out_f32"], r["out_send"], r["out_buf"]
    for c in range(WB):
        out_f32[pl.ds(c, N, stride=WB), :] = expert_out[:, c * LANES : (c + 1) * LANES]
    out_send[...] = out_f32[...].astype(BF16).reshape(N, WB, LANES)

    def row_of(to):
        return to[1] * E + to[0] * EN + to[2]

    to_all(lambda to: send(out_send.at[row_of(to)], out_buf.at[me], 4, to))
    out_buf[me] = out_send[me]
    own_label = r["labels"][...].astype(F32)
    weight_column = gate_weight.reshape(E, 1, 1)
    await_all(out_buf, N - 1, recv_sem.at[4])

    outs = out_buf[0:E].astype(F32)
    for half in range(1, SQ):
        outs += out_buf[half * E : (half + 1) * E].astype(F32)
    final = stream + jnp.sum(outs * weight_column, axis=0)
    scale = lax.rsqrt(total(final * final) * (1.0 / width) + EPSILON)
    along = total(final * head_f32)
    reward = along * scale
    decay = jnp.exp(-jnp.abs(reward))
    row_loss = jnp.maximum(reward, 0.0) + jnp.log1p(decay) - own_label * reward
    error = jnp.where(reward >= 0.0, 1.0, decay) / (1.0 + decay) - own_label
    d_mix = (
        (error * scale) * (head_f32 - final * (scale * scale * along * (1.0 / width)))
    ).astype(BF16).astype(F32)
    grad_send, grad_buf, grad_f32 = r["grad_send"], r["grad_buf"], r["grad_f32"]
    dlog_own, dlog_buf = r["dlog_own"], r["dlog_buf"]
    grad_send[...] = (weight_column * d_mix[None]).astype(BF16)

    to_all(lambda to: send(grad_send.at[to[0] * EN + to[2]], grad_buf.at[me], 5, to))
    grad_buf[me] = grad_send[expert]
    route_dot = jnp.sum(jnp.sum(outs * d_mix[None], axis=1), axis=1, keepdims=True)
    mean_dot = jnp.sum(gate_weight * route_dot, axis=0, keepdims=True)
    d_logits = to_row(gate_weight * (route_dot - mean_dot), E)
    if E < LANES:
        d_logits = jnp.concatenate([d_logits, jnp.zeros((1, LANES - E), F32)], axis=1)
    dlog_own[...] = jnp.concatenate(
        [d_logits, jnp.broadcast_to(row_loss, (1, LANES))], axis=0
    )
    to_all(lambda to: send(dlog_own, dlog_buf.at[me], 6, to))
    dlog_buf[me] = dlog_own[...]
    share = width // N
    first = (mine * EN + ex) * share
    own_columns = norm_f32[pl.ds(first // LANES, N, stride=WB), :]
    own_columns = pltpu.roll(own_columns, lax.rem(LANES - lax.rem(first, LANES), LANES), 1)

    await_all(grad_buf, N - 1, recv_sem.at[5])
    grad_f32[...] = grad_buf[...].astype(F32).reshape(N * WB, LANES)
    for c in range(WB):
        r["grads"][:, c * LANES : (c + 1) * LANES] = grad_f32[
            pl.ds(c, N, stride=WB), :
        ].astype(BF16)
    stores.append(pltpu.make_async_copy(r["grads"], r["out_grads"], load_sem.at[1]))
    stores[-1].start()
    await_all(dlog_buf, N - 1, recv_sem.at[6])
    r["loss"][...] = jnp.sum(dlog_buf[:, 1, :], axis=0, keepdims=True)
    router_grad = lax.dot_general(
        dlog_buf[:, 0, :],
        own_columns,
        (((0,), (0,)), ((), ())),
        precision=lax.Precision.HIGHEST,
        preferred_element_type=F32,
    )
    r["router_grad"][...] = router_grad[0:E, 0:share].astype(BF16)
    stores.append(pltpu.make_async_copy(r["loss"], r["out_loss"], load_sem.at[2]))
    stores[-1].start()
    stores.append(pltpu.make_async_copy(r["router_grad"], r["out_router"], load_sem.at[3]))
    stores[-1].start()

    for number, (buf, count) in enumerate(
        [
            (q_buf, G - 1),
            (part_buf, G - 1),
            (mix_buf, G - 1),
            (norm_buf, N - 1),
            (out_buf, N - 1),
            (grad_buf, N - 1),
            (dlog_buf, N - 1),
        ]
    ):
        await_all(buf, count, send_sem.at[number])
    for store in stores:
        store.wait()


def down_kernel(*refs):
    sources, (loss_out, down_out, router_out), targets = refs[:4], refs[4:7], refs[7:11]
    stage, sem = refs[11:]
    loads = [
        pltpu.make_async_copy(source, target, sem.at[i])
        for i, (source, target) in enumerate(zip(sources, targets))
    ]
    for load in loads:
        load.start()
    for load in loads:
        load.wait()
    hidden, grads, loss, router_grad = targets
    step = stage.shape[1] // 4
    stores = []
    for i in range(4):
        columns = pl.ds(i * step, step)
        stage[:, i * step : (i + 1) * step] = lax.dot_general(
            hidden[...],
            grads[:, i * step : (i + 1) * step],
            (((0,), (0,)), ((), ())),
            preferred_element_type=F32,
        ).astype(BF16)
        stores.append(
            pltpu.make_async_copy(stage.at[:, columns], down_out.at[0, :, columns], sem.at[i])
        )
        stores[-1].start()
    loss_out[...] = loss[:, 0:1]
    router_out[...] = router_grad[...]
    for store in stores:
        store.wait()


def shards(
    sizes,
    keys,
    values,
    queries,
    residual,
    out_proj,
    norm_gain,
    router,
    w_gate,
    w_up,
    w_down,
    head_vec,
    routes,
    step_pos,
    labels,
    trace_len,
):
    DP, SQ, EN = sizes
    G, E = DP * SQ, DP * EN
    N = G * EN
    width = residual.shape[2]
    WB = width // LANES
    hidden_units = w_gate.shape[2]
    hbm = pl.BlockSpec(memory_space=pl.ANY)
    vmem = pl.BlockSpec(memory_space=pltpu.VMEM)
    message = (WB, LANES)
    operands = dict(
        queries=queries[0],
        step_pos=step_pos,
        trace_len=trace_len,
        keys=keys,
        values=values,
        residual=residual[0],
        norm_gain=norm_gain.reshape(message),
        router=router.T,
        head_vec=head_vec.reshape(message),
        routes=routes[0],
        labels=labels,
        out_proj=out_proj,
        w_gate=w_gate,
        w_up=w_up,
        w_down=w_down,
    )
    outs = dict(
        out_loss=jax.ShapeDtypeStruct((1, LANES), F32),
        out_hidden=jax.ShapeDtypeStruct((N, hidden_units), BF16),
        out_grads=jax.ShapeDtypeStruct((N, width), BF16),
        out_router=jax.ShapeDtypeStruct((E, width // N), BF16),
    )
    scratch = {
        name: pltpu.VMEM(operands[name].shape[-2:], operands[name].dtype) for name in INPUTS
    }
    scratch.update(
        loss=pltpu.VMEM((1, LANES), F32),
        hidden=pltpu.VMEM((N, hidden_units), BF16),
        grads=pltpu.VMEM((N, width), BF16),
        router_grad=pltpu.VMEM((E, width // N), BF16),
        q_own=pltpu.VMEM((QUERY_HEADS, LANES), BF16),
        q_buf=pltpu.VMEM((G, QUERY_HEADS, LANES), BF16),
        q_f32=pltpu.VMEM((G * QUERY_HEADS, LANES), F32),
        part_send=pltpu.VMEM((G, QUERY_HEADS + STAT_ROWS, LANES), BF16),
        part_buf=pltpu.VMEM((G, QUERY_HEADS + STAT_ROWS, LANES), BF16),
        mix_f32=pltpu.VMEM((G * WB, LANES), F32),
        mix_send=pltpu.VMEM((G,) + message, BF16),
        mix_buf=pltpu.VMEM((G,) + message, BF16),
        norm_own=pltpu.VMEM(message, BF16),
        norm_buf=pltpu.VMEM((N,) + message, BF16),
        norm_f32=pltpu.VMEM((N * WB, LANES), F32),
        rows=pltpu.VMEM((N, width), BF16),
        out_f32=pltpu.VMEM((N * WB, LANES), F32),
        out_send=pltpu.VMEM((N,) + message, BF16),
        out_buf=pltpu.VMEM((N,) + message, BF16),
        grad_send=pltpu.VMEM((E,) + message, BF16),
        grad_buf=pltpu.VMEM((N,) + message, BF16),
        grad_f32=pltpu.VMEM((N * WB, LANES), F32),
        dlog_own=pltpu.VMEM((2, LANES), F32),
        dlog_buf=pltpu.VMEM((N, 2, LANES), F32),
        load_sem=pltpu.SemaphoreType.DMA((len(INPUTS),)),
        send_sem=pltpu.SemaphoreType.DMA((7,)),
        recv_sem=pltpu.SemaphoreType.DMA((7,)),
    )
    names = ["in_" + name for name in INPUTS] + list(outs) + list(scratch)
    loss, hidden, grads, grad_router = pl.pallas_call(
        functools.partial(kernel, sizes, names),
        out_shape=tuple(outs.values()),
        in_specs=[hbm] * len(INPUTS),
        out_specs=(hbm,) * len(outs),
        scratch_shapes=list(scratch.values()),
        compiler_params=pltpu.CompilerParams(
            collective_id=0, has_side_effects=True, vmem_limit_bytes=56 * 1024 * 1024
        ),
    )(*[operands[name] for name in INPUTS])
    loss, grad_down, grad_router = pl.pallas_call(
        down_kernel,
        out_shape=(
            jax.ShapeDtypeStruct((1, 1), F32),
            jax.ShapeDtypeStruct((1, hidden_units, width), BF16),
            jax.ShapeDtypeStruct((E, width // N), BF16),
        ),
        in_specs=[hbm] * 4,
        out_specs=(vmem, hbm, vmem),
        scratch_shapes=[
            pltpu.VMEM((N, hidden_units), BF16),
            pltpu.VMEM((N, width), BF16),
            pltpu.VMEM((1, LANES), F32),
            pltpu.VMEM((E, width // N), BF16),
            pltpu.VMEM((hidden_units, width), BF16),
            pltpu.SemaphoreType.DMA((4,)),
        ],
        compiler_params=pltpu.CompilerParams(vmem_limit_bytes=60 * 1024 * 1024),
    )(hidden, grads, loss, grad_router)
    return loss.reshape(()), grad_down, grad_router.T


def solution(mesh):
    sizes = (mesh.shape["dp"], mesh.shape["seq"], mesh.shape["expert"])
    return jax.shard_map(
        functools.partial(shards, sizes),
        mesh=mesh,
        in_specs=(
            P("expert", ("dp", "seq"), None),
            P("expert", ("dp", "seq"), None),
            P("expert", ("dp", "seq"), None),
            P("expert", ("dp", "seq"), None),
            P(("dp", "seq"), None),
            P(),
            P(),
            P(("dp", "expert"), None, "seq"),
            P(("dp", "expert"), None, "seq"),
            P(("dp", "expert"), "seq", None),
            P(),
            P("expert", "dp", None),
            P("expert", None),
            P("expert", ("dp", "seq")),
            P("expert", None),
        ),
        out_specs=(P(), P(("dp", "expert"), "seq", None), P(("dp", "seq", "expert"), None)),
        check_vma=False,
    )
```

```python
import functools

import jax
import jax.numpy as jnp
from jax import lax
from jax.experimental import pallas as pl
from jax.experimental.pallas import tpu as pltpu
from jax.sharding import PartitionSpec as P

QUERY_HEADS = 32
KEY_VALUE_HEADS = 4
HEAD_WIDTH = 128
LANES = 128
MASKED = -1e30
EPSILON = 1e-06
STAT_ROWS = 16
INPUTS = (
    "queries",
    "step_pos",
    "trace_len",
    "keys",
    "values",
    "residual",
    "norm_gain",
    "router",
    "head_vec",
    "routes",
    "labels",
    "out_proj",
    "w_gate",
    "w_up",
    "w_down",
)
LARGE = ("out_proj", "w_gate", "w_up", "w_down")
MESH = pl.DeviceIdType.MESH
F32 = jnp.float32
BF16 = jnp.bfloat16


def iota(shape, axis):
    return lax.broadcasted_iota(jnp.int32, shape, axis)


def total(x):
    return jnp.sum(jnp.sum(x, axis=1, keepdims=True), axis=0, keepdims=True)


def to_row(column, n):
    eye = iota((n, n), 0) == iota((n, n), 1)
    return jnp.sum(jnp.where(eye, column, 0.0), axis=0, keepdims=True)


def to_column(row, n):
    eye = iota((n, n), 0) == iota((n, n), 1)
    return jnp.sum(jnp.where(eye, row, 0.0), axis=1, keepdims=True)


def split3(x):
    high = x.astype(BF16).astype(F32)
    rest = x - high
    middle = rest.astype(BF16).astype(F32)
    return [high, middle, rest - middle]


def kernel(sizes, names, *refs):
    r = dict(zip(names, refs))
    DP, SQ, EN = sizes
    G, E = DP * SQ, DP * EN
    N = G * EN
    unroll = N <= 32
    proj_v, gate_v, up_v, down_v = r["out_proj"], r["w_gate"], r["w_up"], r["w_down"]
    width = proj_v.shape[1]
    WB = width // LANES
    dp, sq, ex = lax.axis_index("dp"), lax.axis_index("seq"), lax.axis_index("expert")
    mine = dp * SQ + sq
    block = sq * E + ex * DP
    me = block + dp
    tokens = r["keys"].shape[0]
    load_sem, send_sem, recv_sem = r["load_sem"], r["send_sem"], r["recv_sem"]

    loads = {}
    for i, name in enumerate(INPUTS):
        source, target = r["in_" + name], r[name]
        if len(source.shape) > len(target.shape):
            source = source.at[0]
        loads[name] = pltpu.make_async_copy(source, target, load_sem.at[i])
        if name not in LARGE:
            loads[name].start()

    if unroll:
        near_dp = [lax.rem(dp + a, DP) for a in range(DP)]
        near_sq = [lax.rem(sq + a, SQ) for a in range(SQ)]
        near_ex = [lax.rem(ex + a, EN) for a in range(EN)]

        def near(a, b, c):
            return near_dp[a], near_sq[b], near_ex[c]
    else:

        def near(a, b, c):
            return lax.rem(dp + a, DP), lax.rem(sq + b, SQ), lax.rem(ex + c, EN)

    def each(first, last, body):
        if unroll:
            for i in range(first, last):
                body(i)
        else:

            def step(i, carry):
                body(i)
                return carry

            lax.fori_loop(first, last, step, 0)

    def to_pack(body):
        each(1, G, lambda i: body(near(i // SQ, i % SQ, 0)))

    def along_dp(body):
        each(1, DP, lambda i: body(near(i, 0, 0)))

    def along_expert(body):
        each(1, EN, lambda i: body(near(0, 0, i)))

    def to_pair(body):
        each(1, SQ, lambda i: body(near(0, i, 0)))

    barrier = pltpu.get_barrier_semaphore()

    def greet(to):
        pl.semaphore_signal(barrier, inc=1, device_id=to, device_id_type=MESH)

    to_pack(greet)
    along_expert(greet)
    partners = G - 1 + EN - 1

    def send(source, target, number, to):
        pltpu.make_async_remote_copy(
            src_ref=source,
            dst_ref=target,
            send_sem=send_sem.at[number],
            recv_sem=recv_sem.at[number],
            device_id=to,
            device_id_type=MESH,
        ).start()

    def await_all(buf, count, sem):
        span = buf.at[pl.ds(0, count)]
        pltpu.make_async_copy(span, span, sem).wait()

    q_own, q_buf, q_f32 = r["q_own"], r["q_buf"], r["q_f32"]
    loads["queries"].wait()
    q_row = r["queries"][...].astype(F32)
    q_own[...] = jnp.concatenate(
        [q_row[:, h * LANES : (h + 1) * LANES] for h in range(QUERY_HEADS)], axis=0
    ).astype(BF16)
    pl.semaphore_wait(barrier, partners)

    to_pack(lambda to: send(q_own, q_buf.at[mine], 0, to))
    for name in LARGE:
        loads[name].start()
    q_buf[mine] = q_own[...]

    for name in INPUTS:
        if name != "queries" and name not in LARGE:
            loads[name].wait()
    traces = r["trace_len"].shape[1]
    pos_col = to_column(r["step_pos"][...].astype(F32), G)
    len_row = r["trace_len"][...].astype(F32)
    len_col = to_column(len_row, traces)
    before = iota((traces, traces), 0) <= iota((traces, traces), 1)
    ends_row = jnp.sum(jnp.where(before, len_col, 0.0), axis=0, keepdims=True)
    start_col = jnp.sum(jnp.where(ends_row <= pos_col, len_row, 0.0), axis=1, keepdims=True)
    key_pos = (mine * tokens + iota((G, tokens), 1)).astype(F32)
    allowed = jnp.where((key_pos <= pos_col) & (key_pos >= start_col), 1.0, 0.0)
    group = QUERY_HEADS // KEY_VALUE_HEADS
    allowed = jnp.concatenate([allowed] * group, axis=0) > 0.5
    await_all(q_buf, G - 1, recv_sem.at[0])

    part_send, part_buf = r["part_send"], r["part_buf"]
    key_v, value_v = r["keys"], r["values"]
    q_f32[...] = q_buf[...].astype(F32).reshape(G * QUERY_HEADS, LANES)
    peaks, sums = [], []
    owners = G // KEY_VALUE_HEADS
    for g in range(KEY_VALUE_HEADS):
        q_part = jnp.concatenate(
            [q_f32[pl.ds(g * group + h, G, stride=QUERY_HEADS), :] for h in range(group)], axis=0
        ).astype(BF16)
        columns = slice(g * HEAD_WIDTH, (g + 1) * HEAD_WIDTH)
        score = (
            lax.dot_general(
                q_part, key_v[:, columns], (((1,), (1,)), ((), ())), preferred_element_type=F32
            )
            * HEAD_WIDTH ** (-0.5)
        )
        score = jnp.where(allowed, score, MASKED)
        peak = jnp.max(score, axis=1, keepdims=True)
        weight = jnp.where(allowed, jnp.exp(score - peak), 0.0)
        peaks.append(peak)
        sums.append(jnp.sum(weight, axis=1, keepdims=True))
        part = jnp.dot(weight.astype(BF16), value_v[:, columns], preferred_element_type=F32)
        part_send[g * owners : (g + 1) * owners, 0:QUERY_HEADS] = part.astype(BF16).reshape(
            owners, QUERY_HEADS, LANES
        )
    peaks, sums = jnp.concatenate(peaks, axis=0), jnp.concatenate(sums, axis=0)
    per_block = LANES // QUERY_HEADS
    for b in range(G // per_block):
        span = slice(b * LANES, (b + 1) * LANES)
        stat = jnp.concatenate(
            split3(to_row(peaks[span], LANES))
            + split3(to_row(sums[span], LANES))
            + [jnp.zeros((STAT_ROWS - 6, LANES), F32)],
            axis=0,
        ).astype(BF16)
        part_send[b * per_block : (b + 1) * per_block, QUERY_HEADS:] = jnp.broadcast_to(
            stat[None], (per_block, STAT_ROWS, LANES)
        )

    to_pack(lambda to: send(part_send.at[to[0] * SQ + to[1]], part_buf.at[mine], 1, to))
    part_buf[mine] = part_send[mine]
    loads["out_proj"].wait()
    lane = iota((QUERY_HEADS, LANES), 1)
    pick = lane == lax.rem(mine, per_block) * QUERY_HEADS + iota((QUERY_HEADS, LANES), 0)
    await_all(part_buf, G - 1, recv_sem.at[1])

    peak_of, sum_of = [], []
    for s in range(G):
        stat = part_buf[s, QUERY_HEADS:].astype(F32)
        peak_row = stat[0:1] + stat[1:2] + stat[2:3]
        sum_row = stat[3:4] + stat[4:5] + stat[5:6]
        peak_of.append(jnp.sum(jnp.where(pick, peak_row, 0.0), axis=1, keepdims=True))
        sum_of.append(jnp.sum(jnp.where(pick, sum_row, 0.0), axis=1, keepdims=True))
    peak_all = functools.reduce(jnp.maximum, peak_of)
    weighted = jnp.zeros((QUERY_HEADS, LANES), F32)
    sum_all = jnp.zeros((QUERY_HEADS, 1), F32)
    for s in range(G):
        factor = jnp.exp(peak_of[s] - peak_all)
        weighted += part_buf[s, 0:QUERY_HEADS].astype(F32) * factor
        sum_all += sum_of[s] * factor
    attn = weighted / sum_all
    attn = jnp.concatenate(
        [attn[h * G : (h + 1) * G] for h in range(QUERY_HEADS // G)], axis=1
    ).astype(BF16)
    mixed = jnp.dot(attn, proj_v[...], preferred_element_type=F32)
    mix_f32, mix_send, mix_buf = r["mix_f32"], r["mix_send"], r["mix_buf"]
    for c in range(WB):
        mix_f32[pl.ds(c, G, stride=WB), :] = mixed[:, c * LANES : (c + 1) * LANES]
    mix_send[...] = mix_f32[...].astype(BF16).reshape(G, WB, LANES)

    to_pack(lambda to: send(mix_send.at[to[0] * SQ + to[1]], mix_buf.at[mine], 2, to))
    mix_buf[mine] = mix_send[mine]
    res_row = r["residual"][...].astype(F32)
    stream = jnp.concatenate(
        [res_row[:, c * LANES : (c + 1) * LANES] for c in range(WB)], axis=0
    )
    head_f32 = r["head_vec"][...].astype(F32)
    gain = r["norm_gain"][...].astype(F32)
    await_all(mix_buf, G - 1, recv_sem.at[2])
    stream += jnp.sum(mix_buf[...].astype(F32), axis=0)
    scale = lax.rsqrt(total(stream * stream) * (1.0 / width) + EPSILON)
    normed = (stream * scale * gain).astype(BF16)
    norm_own, norm_buf, norm_f32, rows = r["norm_own"], r["norm_buf"], r["norm_f32"], r["rows"]
    norm_own[...] = normed

    line, plane = pl.ds(block, DP), pl.ds(sq * E, E)
    along_dp(lambda to: send(norm_own, norm_buf.at[me], 3, to))
    norm_buf[me] = norm_own[...]

    await_all(norm_buf, DP - 1, recv_sem.at[3])
    along_expert(lambda to: send(norm_buf.at[line], norm_buf.at[line], 4, to))

    normed = normed.astype(F32)
    logits = jnp.zeros((E, LANES), F32)
    for c in range(WB):
        logits += r["router"][:, c * LANES : (c + 1) * LANES].astype(F32) * normed[c : c + 1]
    logits = jnp.sum(logits, axis=1, keepdims=True)
    route_row = r["routes"][pl.ds(sq, 1), :].astype(F32)
    topk = r["routes"].shape[1]
    chosen = jnp.sum(
        jnp.where(iota((E, topk), 0).astype(F32) == route_row, 1.0, 0.0), axis=1, keepdims=True
    )
    masked = jnp.where(chosen > 0.5, logits, MASKED)
    power = jnp.where(
        chosen > 0.5, jnp.exp(masked - jnp.max(masked, axis=0, keepdims=True)), 0.0
    )
    gate_weight = power / jnp.sum(power, axis=0, keepdims=True)

    await_all(norm_buf, E - DP, recv_sem.at[4])
    to_pair(lambda to: send(norm_buf.at[plane], norm_buf.at[plane], 5, to))
    for name in ("w_gate", "w_up", "w_down"):
        loads[name].wait()
    await_all(norm_buf, N - E, recv_sem.at[5])

    norm_f32[...] = norm_buf[...].astype(F32).reshape(N * WB, LANES)
    for c in range(WB):
        rows[:, c * LANES : (c + 1) * LANES] = norm_f32[pl.ds(c, N, stride=WB), :].astype(BF16)
    gate_act = jnp.dot(rows[...], gate_v[...], preferred_element_type=F32)
    up_act = jnp.dot(rows[...], up_v[...], preferred_element_type=F32)
    hidden = (gate_act / (1.0 + jnp.exp(-gate_act)) * up_act).astype(BF16)
    r["hidden"][...] = hidden
    stores = [pltpu.make_async_copy(r["hidden"], r["out_hidden"], load_sem.at[0])]
    stores[0].start()
    expert_out = jnp.dot(hidden, down_v[...], preferred_element_type=F32)
    out_f32, half_send, half_buf = r["out_f32"], r["half_send"], r["half_buf"]
    out_send, out_buf = r["out_send"], r["out_buf"]
    for c in range(WB):
        out_f32[pl.ds(c, N, stride=WB), :] = expert_out[:, c * LANES : (c + 1) * LANES]
    half_send[...] = out_f32[...].astype(BF16).reshape(SQ, E, WB, LANES)

    to_pair(lambda to: send(half_send.at[to[1]], half_buf.at[sq], 6, to))
    await_all(half_buf, SQ - 1, recv_sem.at[6])
    outs = out_f32[pl.ds(pl.multiple_of(sq * (E * WB), E * WB), E * WB), :].reshape(E, WB, LANES)
    for i in range(1, SQ):
        outs += half_buf[lax.rem(sq + i, SQ)].astype(F32)
    out_send[...] = outs.astype(BF16).reshape(EN, DP, WB, LANES)
    out_mid = r["out_mid"]
    along_expert(lambda to: send(out_send.at[to[2]], out_mid.at[ex], 7, to))
    out_mid[ex] = out_send[ex]
    await_all(out_mid, EN - 1, recv_sem.at[7])
    along_dp(lambda to: send(out_mid.at[:, to[0]], out_buf.at[dp], 8, to))
    for c in range(EN):
        out_buf[dp, c] = out_mid[c, dp]
    own_label = r["labels"][...].astype(F32)
    weight_column = gate_weight.reshape(E, 1, 1)
    await_all(out_buf, DP - 1, recv_sem.at[8])

    outs = out_buf[...].astype(F32).reshape(E, WB, LANES)
    final = stream + jnp.sum(outs * weight_column, axis=0)
    scale = lax.rsqrt(total(final * final) * (1.0 / width) + EPSILON)
    along = total(final * head_f32)
    reward = along * scale
    decay = jnp.exp(-jnp.abs(reward))
    row_loss = jnp.maximum(reward, 0.0) + jnp.log1p(decay) - own_label * reward
    error = jnp.where(reward >= 0.0, 1.0, decay) / (1.0 + decay) - own_label
    d_mix = (
        (error * scale) * (head_f32 - final * (scale * scale * along * (1.0 / width)))
    ).astype(BF16).astype(F32)
    grad_send, grad_buf, grad_f32 = r["grad_send"], r["grad_buf"], r["grad_f32"]
    dlog_own, dlog_buf = r["dlog_own"], r["dlog_buf"]
    grad_send[...] = (weight_column * d_mix[None]).astype(BF16).reshape(DP, EN, WB, LANES)

    grad_mid = r["grad_mid"]
    along_dp(lambda to: send(grad_send.at[to[0]], grad_mid.at[dp], 9, to))
    grad_mid[dp] = grad_send[dp]
    route_dot = jnp.sum(jnp.sum(outs * d_mix[None], axis=1), axis=1, keepdims=True)
    mean_dot = jnp.sum(gate_weight * route_dot, axis=0, keepdims=True)
    d_logits = to_row(gate_weight * (route_dot - mean_dot), E)
    if E < LANES:
        d_logits = jnp.concatenate([d_logits, jnp.zeros((1, LANES - E), F32)], axis=1)
    dlog_own[...] = jnp.concatenate(
        [d_logits, jnp.broadcast_to(row_loss, (1, LANES))], axis=0
    )
    along_dp(lambda to: send(dlog_own, dlog_buf.at[me], 12, to))
    dlog_buf[me] = dlog_own[...]
    await_all(grad_mid, DP - 1, recv_sem.at[9])
    along_expert(lambda to: send(grad_mid.at[:, to[2]], grad_buf.at[line], 10, to))
    for a in range(DP):
        grad_buf[block + a] = grad_mid[a, ex]
    await_all(dlog_buf, DP - 1, recv_sem.at[12])
    along_expert(lambda to: send(dlog_buf.at[line], dlog_buf.at[line], 13, to))
    share = width // N
    first = (mine * EN + ex) * share
    own_columns = norm_f32[pl.ds(first // LANES, N, stride=WB), :]
    own_columns = pltpu.roll(own_columns, lax.rem(LANES - lax.rem(first, LANES), LANES), 1)

    await_all(grad_buf, E - DP, recv_sem.at[10])
    to_pair(lambda to: send(grad_buf.at[plane], grad_buf.at[plane], 11, to))
    await_all(dlog_buf, E - DP, recv_sem.at[13])
    to_pair(lambda to: send(dlog_buf.at[plane], dlog_buf.at[plane], 14, to))
    await_all(grad_buf, N - E, recv_sem.at[11])
    grad_f32[...] = grad_buf[...].astype(F32).reshape(N * WB, LANES)
    for c in range(WB):
        r["grads"][:, c * LANES : (c + 1) * LANES] = grad_f32[
            pl.ds(c, N, stride=WB), :
        ].astype(BF16)
    stores.append(pltpu.make_async_copy(r["grads"], r["out_grads"], load_sem.at[1]))
    stores[-1].start()
    await_all(dlog_buf, N - E, recv_sem.at[14])
    r["loss"][...] = jnp.sum(dlog_buf[:, 1, :], axis=0, keepdims=True)
    router_grad = lax.dot_general(
        dlog_buf[:, 0, :],
        own_columns,
        (((0,), (0,)), ((), ())),
        precision=lax.Precision.HIGHEST,
        preferred_element_type=F32,
    )
    r["router_grad"][...] = router_grad[0:E, 0:share].astype(BF16)
    stores.append(pltpu.make_async_copy(r["loss"], r["out_loss"], load_sem.at[2]))
    stores[-1].start()
    stores.append(pltpu.make_async_copy(r["router_grad"], r["out_router"], load_sem.at[3]))
    stores[-1].start()

    for number, (buf, count) in enumerate(
        [
            (q_buf, G - 1),
            (part_buf, G - 1),
            (mix_buf, G - 1),
            (norm_buf, DP - 1),
            (norm_buf, E - DP),
            (norm_buf, N - E),
            (half_buf, SQ - 1),
            (out_mid, EN - 1),
            (out_buf, DP - 1),
            (grad_mid, DP - 1),
            (grad_buf, E - DP),
            (grad_buf, N - E),
            (dlog_buf, DP - 1),
            (dlog_buf, E - DP),
            (dlog_buf, N - E),
        ]
    ):
        await_all(buf, count, send_sem.at[number])
    for store in stores:
        store.wait()


def down_kernel(*refs):
    sources, (loss_out, down_out, router_out), targets = refs[:4], refs[4:7], refs[7:11]
    stage, sem = refs[11:]
    loads = [
        pltpu.make_async_copy(source, target, sem.at[i])
        for i, (source, target) in enumerate(zip(sources, targets))
    ]
    for load in loads:
        load.start()
    for load in loads:
        load.wait()
    hidden, grads, loss, router_grad = targets
    step = stage.shape[1] // 4
    stores = []
    for i in range(4):
        columns = pl.ds(i * step, step)
        stage[:, i * step : (i + 1) * step] = lax.dot_general(
            hidden[...],
            grads[:, i * step : (i + 1) * step],
            (((0,), (0,)), ((), ())),
            preferred_element_type=F32,
        ).astype(BF16)
        stores.append(
            pltpu.make_async_copy(stage.at[:, columns], down_out.at[0, :, columns], sem.at[i])
        )
        stores[-1].start()
    loss_out[...] = loss[:, 0:1]
    router_out[...] = router_grad[...]
    for store in stores:
        store.wait()


def shards(
    sizes,
    keys,
    values,
    queries,
    residual,
    out_proj,
    norm_gain,
    router,
    w_gate,
    w_up,
    w_down,
    head_vec,
    routes,
    step_pos,
    labels,
    trace_len,
):
    DP, SQ, EN = sizes
    G, E = DP * SQ, DP * EN
    N = G * EN
    width = residual.shape[2]
    WB = width // LANES
    hidden_units = w_gate.shape[2]
    hbm = pl.BlockSpec(memory_space=pl.ANY)
    vmem = pl.BlockSpec(memory_space=pltpu.VMEM)
    message = (WB, LANES)
    operands = dict(
        queries=queries[0],
        step_pos=step_pos,
        trace_len=trace_len,
        keys=keys,
        values=values,
        residual=residual[0],
        norm_gain=norm_gain.reshape(message),
        router=router.T,
        head_vec=head_vec.reshape(message),
        routes=routes[0],
        labels=labels,
        out_proj=out_proj,
        w_gate=w_gate,
        w_up=w_up,
        w_down=w_down,
    )
    outs = dict(
        out_loss=jax.ShapeDtypeStruct((1, LANES), F32),
        out_hidden=jax.ShapeDtypeStruct((N, hidden_units), BF16),
        out_grads=jax.ShapeDtypeStruct((N, width), BF16),
        out_router=jax.ShapeDtypeStruct((E, width // N), BF16),
    )
    scratch = {
        name: pltpu.VMEM(operands[name].shape[-2:], operands[name].dtype) for name in INPUTS
    }
    scratch.update(
        loss=pltpu.VMEM((1, LANES), F32),
        hidden=pltpu.VMEM((N, hidden_units), BF16),
        grads=pltpu.VMEM((N, width), BF16),
        router_grad=pltpu.VMEM((E, width // N), BF16),
        q_own=pltpu.VMEM((QUERY_HEADS, LANES), BF16),
        q_buf=pltpu.VMEM((G, QUERY_HEADS, LANES), BF16),
        q_f32=pltpu.VMEM((G * QUERY_HEADS, LANES), F32),
        part_send=pltpu.VMEM((G, QUERY_HEADS + STAT_ROWS, LANES), BF16),
        part_buf=pltpu.VMEM((G, QUERY_HEADS + STAT_ROWS, LANES), BF16),
        mix_f32=pltpu.VMEM((G * WB, LANES), F32),
        mix_send=pltpu.VMEM((G,) + message, BF16),
        mix_buf=pltpu.VMEM((G,) + message, BF16),
        norm_own=pltpu.VMEM(message, BF16),
        norm_buf=pltpu.VMEM((N,) + message, BF16),
        norm_f32=pltpu.VMEM((N * WB, LANES), F32),
        rows=pltpu.VMEM((N, width), BF16),
        out_f32=pltpu.VMEM((N * WB, LANES), F32),
        half_send=pltpu.VMEM((SQ, E) + message, BF16),
        half_buf=pltpu.VMEM((SQ, E) + message, BF16),
        out_send=pltpu.VMEM((EN, DP) + message, BF16),
        out_mid=pltpu.VMEM((EN, DP) + message, BF16),
        out_buf=pltpu.VMEM((DP, EN) + message, BF16),
        grad_send=pltpu.VMEM((DP, EN) + message, BF16),
        grad_mid=pltpu.VMEM((DP, EN) + message, BF16),
        grad_buf=pltpu.VMEM((N,) + message, BF16),
        grad_f32=pltpu.VMEM((N * WB, LANES), F32),
        dlog_own=pltpu.VMEM((2, LANES), F32),
        dlog_buf=pltpu.VMEM((N, 2, LANES), F32),
        load_sem=pltpu.SemaphoreType.DMA((len(INPUTS),)),
        send_sem=pltpu.SemaphoreType.DMA((15,)),
        recv_sem=pltpu.SemaphoreType.DMA((15,)),
    )
    names = ["in_" + name for name in INPUTS] + list(outs) + list(scratch)
    loss, hidden, grads, grad_router = pl.pallas_call(
        functools.partial(kernel, sizes, names),
        out_shape=tuple(outs.values()),
        in_specs=[hbm] * len(INPUTS),
        out_specs=(hbm,) * len(outs),
        scratch_shapes=list(scratch.values()),
        compiler_params=pltpu.CompilerParams(
            collective_id=0, has_side_effects=True, vmem_limit_bytes=56 * 1024 * 1024
        ),
    )(*[operands[name] for name in INPUTS])
    loss, grad_down, grad_router = pl.pallas_call(
        down_kernel,
        out_shape=(
            jax.ShapeDtypeStruct((1, 1), F32),
            jax.ShapeDtypeStruct((1, hidden_units, width), BF16),
            jax.ShapeDtypeStruct((E, width // N), BF16),
        ),
        in_specs=[hbm] * 4,
        out_specs=(vmem, hbm, vmem),
        scratch_shapes=[
            pltpu.VMEM((N, hidden_units), BF16),
            pltpu.VMEM((N, width), BF16),
            pltpu.VMEM((1, LANES), F32),
            pltpu.VMEM((E, width // N), BF16),
            pltpu.VMEM((hidden_units, width), BF16),
            pltpu.SemaphoreType.DMA((4,)),
        ],
        compiler_params=pltpu.CompilerParams(vmem_limit_bytes=60 * 1024 * 1024),
    )(hidden, grads, loss, grad_router)
    return loss.reshape(()), grad_down, grad_router.T


def solution(mesh):
    sizes = (mesh.shape["dp"], mesh.shape["seq"], mesh.shape["expert"])
    return jax.shard_map(
        functools.partial(shards, sizes),
        mesh=mesh,
        in_specs=(
            P("expert", ("dp", "seq"), None),
            P("expert", ("dp", "seq"), None),
            P("expert", ("dp", "seq"), None),
            P("expert", ("dp", "seq"), None),
            P(("dp", "seq"), None),
            P(),
            P(),
            P(("dp", "expert"), None, "seq"),
            P(("dp", "expert"), None, "seq"),
            P(("dp", "expert"), "seq", None),
            P(),
            P("expert", "dp", None),
            P("expert", None),
            P("expert", ("dp", "seq")),
            P("expert", None),
        ),
        out_specs=(P(), P(("dp", "expert"), "seq", None), P(("dp", "seq", "expert"), None)),
        check_vma=False,
    )
```

```python
import functools
import itertools

import jax
import jax.numpy as jnp
from jax import lax
from jax.experimental import pallas as pl
from jax.experimental.pallas import tpu as pltpu
from jax.sharding import PartitionSpec as P

QUERY_HEADS = 32
KEY_VALUE_HEADS = 4
HEAD_WIDTH = 128
LANES = 128
MASKED = -1e30
EPSILON = 1e-06
STAT_ROWS = 16
INPUTS = (
    "queries",
    "step_pos",
    "trace_len",
    "keys",
    "values",
    "residual",
    "norm_gain",
    "router",
    "head_vec",
    "routes",
    "labels",
    "out_proj",
    "w_gate",
    "w_up",
    "w_down",
)
MESH = pl.DeviceIdType.MESH
F32 = jnp.float32
BF16 = jnp.bfloat16


def iota(shape, axis):
    return lax.broadcasted_iota(jnp.int32, shape, axis)


def total(x):
    return jnp.sum(jnp.sum(x, axis=1, keepdims=True), axis=0, keepdims=True)


def to_row(column, n):
    eye = iota((n, n), 0) == iota((n, n), 1)
    return jnp.sum(jnp.where(eye, column, 0.0), axis=0, keepdims=True)


def to_column(row, n):
    eye = iota((n, n), 0) == iota((n, n), 1)
    return jnp.sum(jnp.where(eye, row, 0.0), axis=1, keepdims=True)


def split3(x):
    high = x.astype(BF16).astype(F32)
    rest = x - high
    middle = rest.astype(BF16).astype(F32)
    return [high, middle, rest - middle]


def kernel(sizes, names, *refs):
    r = dict(zip(names, refs))
    DP, SQ, EN = sizes
    G, E = DP * SQ, DP * EN
    N = G * EN
    unroll = N <= 32
    proj_v, gate_v, up_v, down_v = r["out_proj"], r["w_gate"], r["w_up"], r["w_down"]
    width = proj_v.shape[1]
    WB = width // LANES
    dp, sq, ex = lax.axis_index("dp"), lax.axis_index("seq"), lax.axis_index("expert")
    mine = dp * SQ + sq
    expert = dp * EN + ex
    me = sq * E + expert
    tokens = r["keys"].shape[0]
    load_sem, send_sem, recv_sem = r["load_sem"], r["send_sem"], r["recv_sem"]

    loads = {}
    for i, name in enumerate(INPUTS):
        source, target = r["in_" + name], r[name]
        if len(source.shape) > len(target.shape):
            source = source.at[0]
        loads[name] = pltpu.make_async_copy(source, target, load_sem.at[i])
        loads[name].start()

    if unroll:
        near_dp = [lax.rem(dp + a, DP) for a in range(DP)]
        near_sq = [lax.rem(sq + a, SQ) for a in range(SQ)]
        near_ex = [lax.rem(ex + a, EN) for a in range(EN)]

        def near(a, b, c):
            return near_dp[a], near_sq[b], near_ex[c]
    else:

        def near(a, b, c):
            return lax.rem(dp + a, DP), lax.rem(sq + b, SQ), lax.rem(ex + c, EN)

    far_first = sorted(range(DP), key=lambda a: abs(a - DP // 2))

    def each(first, last, body):
        if unroll:
            for i in range(first, last):
                body(i)
        else:

            def step(i, carry):
                body(i)
                return carry

            lax.fori_loop(first, last, step, 0)

    def to_pack(body):
        if unroll:
            for a, b in itertools.product(far_first, range(SQ)):
                if a or b:
                    body(near(a, b, 0))
        else:
            each(1, G, lambda i: body(near(i // SQ, i % SQ, 0)))

    def to_plane(body):
        if unroll:
            for a, c in itertools.product(far_first, range(EN)):
                if a or c:
                    body(near(a, 0, c))
        else:
            each(1, E, lambda i: body(near(i // EN, 0, i % EN)))

    def to_pair(body):
        each(1, SQ, lambda i: body(near(0, i, 0)))

    barrier = pltpu.get_barrier_semaphore()

    def greet(to):
        pl.semaphore_signal(barrier, inc=1, device_id=to, device_id_type=MESH)

    to_pack(greet)
    each(1, EN, lambda c: each(0, DP, lambda a: greet(near(a, 0, c))))
    partners = G - 1 + (EN - 1) * DP

    def send(source, target, number, to):
        pltpu.make_async_remote_copy(
            src_ref=source,
            dst_ref=target,
            send_sem=send_sem.at[number],
            recv_sem=recv_sem.at[number],
            device_id=to,
            device_id_type=MESH,
        ).start()

    def await_all(buf, count, sem):
        span = buf.at[pl.ds(0, count)]
        pltpu.make_async_copy(span, span, sem).wait()

    q_own, q_buf, q_f32 = r["q_own"], r["q_buf"], r["q_f32"]
    loads["queries"].wait()
    q_row = r["queries"][...].astype(F32)
    q_own[...] = jnp.concatenate(
        [q_row[:, h * LANES : (h + 1) * LANES] for h in range(QUERY_HEADS)], axis=0
    ).astype(BF16)
    pl.semaphore_wait(barrier, partners)

    to_pack(lambda to: send(q_own, q_buf.at[mine], 0, to))
    q_buf[mine] = q_own[...]

    for name in INPUTS:
        if name not in ("queries", "out_proj", "w_gate", "w_up", "w_down"):
            loads[name].wait()
    traces = r["trace_len"].shape[1]
    pos_col = to_column(r["step_pos"][...].astype(F32), G)
    len_row = r["trace_len"][...].astype(F32)
    len_col = to_column(len_row, traces)
    before = iota((traces, traces), 0) <= iota((traces, traces), 1)
    ends_row = jnp.sum(jnp.where(before, len_col, 0.0), axis=0, keepdims=True)
    start_col = jnp.sum(jnp.where(ends_row <= pos_col, len_row, 0.0), axis=1, keepdims=True)
    key_pos = (mine * tokens + iota((G, tokens), 1)).astype(F32)
    allowed = jnp.where((key_pos <= pos_col) & (key_pos >= start_col), 1.0, 0.0)
    group = QUERY_HEADS // KEY_VALUE_HEADS
    allowed = jnp.concatenate([allowed] * group, axis=0) > 0.5
    await_all(q_buf, G - 1, recv_sem.at[0])

    part_send, part_buf = r["part_send"], r["part_buf"]
    key_v, value_v = r["keys"], r["values"]
    q_f32[...] = q_buf[...].astype(F32).reshape(G * QUERY_HEADS, LANES)
    peaks, sums = [], []
    owners = G // KEY_VALUE_HEADS
    for g in range(KEY_VALUE_HEADS):
        q_part = jnp.concatenate(
            [q_f32[pl.ds(g * group + h, G, stride=QUERY_HEADS), :] for h in range(group)], axis=0
        ).astype(BF16)
        columns = slice(g * HEAD_WIDTH, (g + 1) * HEAD_WIDTH)
        score = (
            lax.dot_general(
                q_part, key_v[:, columns], (((1,), (1,)), ((), ())), preferred_element_type=F32
            )
            * HEAD_WIDTH ** (-0.5)
        )
        score = jnp.where(allowed, score, MASKED)
        peak = jnp.max(score, axis=1, keepdims=True)
        weight = jnp.where(allowed, jnp.exp(score - peak), 0.0)
        peaks.append(peak)
        sums.append(jnp.sum(weight, axis=1, keepdims=True))
        part = jnp.dot(weight.astype(BF16), value_v[:, columns], preferred_element_type=F32)
        part_send[g * owners : (g + 1) * owners, 0:QUERY_HEADS] = part.astype(BF16).reshape(
            owners, QUERY_HEADS, LANES
        )
    peaks, sums = jnp.concatenate(peaks, axis=0), jnp.concatenate(sums, axis=0)
    per_block = LANES // QUERY_HEADS
    for b in range(G // per_block):
        span = slice(b * LANES, (b + 1) * LANES)
        stat = jnp.concatenate(
            split3(to_row(peaks[span], LANES))
            + split3(to_row(sums[span], LANES))
            + [jnp.zeros((STAT_ROWS - 6, LANES), F32)],
            axis=0,
        ).astype(BF16)
        part_send[b * per_block : (b + 1) * per_block, QUERY_HEADS:] = jnp.broadcast_to(
            stat[None], (per_block, STAT_ROWS, LANES)
        )

    to_pack(lambda to: send(part_send.at[to[0] * SQ + to[1]], part_buf.at[mine], 1, to))
    part_buf[mine] = part_send[mine]
    loads["out_proj"].wait()
    lane = iota((QUERY_HEADS, LANES), 1)
    pick = lane == lax.rem(mine, per_block) * QUERY_HEADS + iota((QUERY_HEADS, LANES), 0)
    await_all(part_buf, G - 1, recv_sem.at[1])

    stats = [part_buf[s, QUERY_HEADS:].astype(F32) for s in range(G)]
    peak_rows = jnp.concatenate([t[0:1] + t[1:2] + t[2:3] for t in stats], axis=0)
    sum_rows = jnp.concatenate([t[3:4] + t[4:5] + t[5:6] for t in stats], axis=0)
    factors = jnp.exp(peak_rows - jnp.max(peak_rows, axis=0, keepdims=True))
    factors = factors / jnp.sum(sum_rows * factors, axis=0, keepdims=True)
    attn = jnp.zeros((QUERY_HEADS, LANES), F32)
    for s in range(G):
        factor = jnp.sum(jnp.where(pick, factors[s : s + 1], 0.0), axis=1, keepdims=True)
        attn += part_buf[s, 0:QUERY_HEADS].astype(F32) * factor
    attn = jnp.concatenate(
        [attn[h * G : (h + 1) * G] for h in range(QUERY_HEADS // G)], axis=1
    ).astype(BF16)
    mixed = jnp.dot(attn, proj_v[...], preferred_element_type=F32)
    mix_f32, mix_send, mix_buf = r["mix_f32"], r["mix_send"], r["mix_buf"]
    for c in range(WB):
        mix_f32[pl.ds(c, G, stride=WB), :] = mixed[:, c * LANES : (c + 1) * LANES]
    mix_send[...] = mix_f32[...].astype(BF16).reshape(G, WB, LANES)

    to_pack(lambda to: send(mix_send.at[to[0] * SQ + to[1]], mix_buf.at[mine], 2, to))
    mix_buf[mine] = mix_send[mine]
    res_row = r["residual"][...].astype(F32)
    stream = jnp.concatenate(
        [res_row[:, c * LANES : (c + 1) * LANES] for c in range(WB)], axis=0
    )
    head_f32 = r["head_vec"][...].astype(F32)
    gain = r["norm_gain"][...].astype(F32)
    await_all(mix_buf, G - 1, recv_sem.at[2])
    stream += jnp.sum(mix_buf[...].astype(F32), axis=0)
    scale = lax.rsqrt(total(stream * stream) * (1.0 / width) + EPSILON)
    normed = (stream * scale * gain).astype(BF16)
    norm_own, norm_buf, norm_f32, rows = r["norm_own"], r["norm_buf"], r["norm_f32"], r["rows"]
    norm_own[...] = normed

    to_plane(lambda to: send(norm_own, norm_buf.at[me], 3, to))
    norm_buf[me] = norm_own[...]
    plane = pl.ds(sq * E, E)

    normed = normed.astype(F32)
    logits = jnp.zeros((E, LANES), F32)
    for c in range(WB):
        logits += r["router"][:, c * LANES : (c + 1) * LANES].astype(F32) * normed[c : c + 1]
    logits = jnp.sum(logits, axis=1, keepdims=True)
    route_row = r["routes"][pl.ds(sq, 1), :].astype(F32)
    topk = r["routes"].shape[1]
    chosen = jnp.sum(
        jnp.where(iota((E, topk), 0).astype(F32) == route_row, 1.0, 0.0), axis=1, keepdims=True
    )
    masked = jnp.where(chosen > 0.5, logits, MASKED)
    power = jnp.where(
        chosen > 0.5, jnp.exp(masked - jnp.max(masked, axis=0, keepdims=True)), 0.0
    )
    gate_weight = power / jnp.sum(power, axis=0, keepdims=True)

    await_all(norm_buf, E - 1, recv_sem.at[3])
    to_pair(lambda to: send(norm_buf.at[plane], norm_buf.at[plane], 4, to))
    for name in ("w_gate", "w_up", "w_down"):
        loads[name].wait()
    await_all(norm_buf, N - E, recv_sem.at[4])

    norm_f32[...] = norm_buf[...].astype(F32).reshape(N * WB, LANES)
    for c in range(WB):
        rows[:, c * LANES : (c + 1) * LANES] = norm_f32[pl.ds(c, N, stride=WB), :].astype(BF16)
    gate_act = jnp.dot(rows[...], gate_v[...], preferred_element_type=F32)
    up_act = jnp.dot(rows[...], up_v[...], preferred_element_type=F32)
    hidden = (gate_act / (1.0 + jnp.exp(-gate_act)) * up_act).astype(BF16)
    r["hidden"][...] = hidden
    stores = [pltpu.make_async_copy(r["hidden"], r["out_hidden"], load_sem.at[0])]
    stores[0].start()
    expert_out = jnp.dot(hidden, down_v[...], preferred_element_type=F32)
    out_f32, half_send, half_buf = r["out_f32"], r["half_send"], r["half_buf"]
    out_send, out_buf = r["out_send"], r["out_buf"]
    for c in range(WB):
        out_f32[pl.ds(c, N, stride=WB), :] = expert_out[:, c * LANES : (c + 1) * LANES]
    half_send[...] = out_f32[...].astype(BF16).reshape(SQ, E, WB, LANES)

    to_pair(lambda to: send(half_send.at[to[1]], half_buf.at[sq], 5, to))
    await_all(half_buf, SQ - 1, recv_sem.at[5])
    outs = out_f32[pl.ds(pl.multiple_of(sq * (E * WB), E * WB), E * WB), :].reshape(E, WB, LANES)
    for i in range(1, SQ):
        outs += half_buf[lax.rem(sq + i, SQ)].astype(F32)
    out_send[...] = outs.astype(BF16)
    to_plane(lambda to: send(out_send.at[to[0] * EN + to[2]], out_buf.at[expert], 6, to))
    out_buf[expert] = out_send[expert]
    own_label = r["labels"][...].astype(F32)
    weight_column = gate_weight.reshape(E, 1, 1)
    await_all(out_buf, E - 1, recv_sem.at[6])

    outs = out_buf[...].astype(F32)
    final = stream + jnp.sum(outs * weight_column, axis=0)
    scale = lax.rsqrt(total(final * final) * (1.0 / width) + EPSILON)
    along = total(final * head_f32)
    reward = along * scale
    decay = jnp.exp(-jnp.abs(reward))
    row_loss = jnp.maximum(reward, 0.0) + jnp.log1p(decay) - own_label * reward
    error = jnp.where(reward >= 0.0, 1.0, decay) / (1.0 + decay) - own_label
    d_mix = (
        (error * scale) * (head_f32 - final * (scale * scale * along * (1.0 / width)))
    ).astype(BF16).astype(F32)
    grad_send, grad_buf, grad_f32 = r["grad_send"], r["grad_buf"], r["grad_f32"]
    dlog_own, dlog_buf = r["dlog_own"], r["dlog_buf"]
    grad_send[...] = (weight_column * d_mix[None]).astype(BF16)

    to_plane(lambda to: send(grad_send.at[to[0] * EN + to[2]], grad_buf.at[me], 7, to))
    grad_buf[me] = grad_send[expert]
    route_dot = jnp.sum(jnp.sum(outs * d_mix[None], axis=1), axis=1, keepdims=True)
    mean_dot = jnp.sum(gate_weight * route_dot, axis=0, keepdims=True)
    d_logits = to_row(gate_weight * (route_dot - mean_dot), E)
    if E < LANES:
        d_logits = jnp.concatenate([d_logits, jnp.zeros((1, LANES - E), F32)], axis=1)
    dlog_own[...] = jnp.concatenate(
        [d_logits, jnp.broadcast_to(row_loss, (1, LANES))], axis=0
    )
    to_plane(lambda to: send(dlog_own, dlog_buf.at[me], 9, to))
    dlog_buf[me] = dlog_own[...]
    share = width // N
    first = (mine * EN + ex) * share
    own_columns = norm_f32[pl.ds(first // LANES, N, stride=WB), :]
    own_columns = pltpu.roll(own_columns, lax.rem(LANES - lax.rem(first, LANES), LANES), 1)

    await_all(grad_buf, E - 1, recv_sem.at[7])
    to_pair(lambda to: send(grad_buf.at[plane], grad_buf.at[plane], 8, to))
    await_all(dlog_buf, E - 1, recv_sem.at[9])
    to_pair(lambda to: send(dlog_buf.at[plane], dlog_buf.at[plane], 10, to))
    await_all(grad_buf, N - E, recv_sem.at[8])
    grad_f32[...] = grad_buf[...].astype(F32).reshape(N * WB, LANES)
    for c in range(WB):
        r["grads"][:, c * LANES : (c + 1) * LANES] = grad_f32[
            pl.ds(c, N, stride=WB), :
        ].astype(BF16)
    stores.append(pltpu.make_async_copy(r["grads"], r["out_grads"], load_sem.at[1]))
    stores[-1].start()
    await_all(dlog_buf, N - E, recv_sem.at[10])
    r["loss"][...] = jnp.sum(dlog_buf[:, 1, :], axis=0, keepdims=True)
    router_grad = lax.dot_general(
        dlog_buf[:, 0, :],
        own_columns,
        (((0,), (0,)), ((), ())),
        precision=lax.Precision.HIGHEST,
        preferred_element_type=F32,
    )
    r["router_grad"][...] = router_grad[0:E, 0:share].astype(BF16)
    stores.append(pltpu.make_async_copy(r["loss"], r["out_loss"], load_sem.at[2]))
    stores[-1].start()
    stores.append(pltpu.make_async_copy(r["router_grad"], r["out_router"], load_sem.at[3]))
    stores[-1].start()

    for number, (buf, count) in enumerate(
        [
            (q_buf, G - 1),
            (part_buf, G - 1),
            (mix_buf, G - 1),
            (norm_buf, E - 1),
            (norm_buf, N - E),
            (half_buf, SQ - 1),
            (out_buf, E - 1),
            (grad_buf, E - 1),
            (grad_buf, N - E),
            (dlog_buf, E - 1),
            (dlog_buf, N - E),
        ]
    ):
        await_all(buf, count, send_sem.at[number])
    for store in stores:
        store.wait()


def down_kernel(
    hidden, grads, loss, router_grad, loss_out, down_out, router_out, rows, columns, stage, sem
):
    loads = [
        pltpu.make_async_copy(hidden, rows, sem.at[4]),
        pltpu.make_async_copy(grads, columns, sem.at[5]),
    ]
    passes = [
        pltpu.make_async_copy(loss, loss_out, sem.at[6]),
        pltpu.make_async_copy(router_grad, router_out, sem.at[7]),
    ]
    for copy in loads + passes:
        copy.start()
    for load in loads:
        load.wait()
    step = stage.shape[1] // 4
    stores = []
    for i in range(4):
        span = pl.ds(i * step, step)
        stage[:, i * step : (i + 1) * step] = lax.dot_general(
            rows[...],
            columns[:, i * step : (i + 1) * step],
            (((0,), (0,)), ((), ())),
            preferred_element_type=F32,
        ).astype(BF16)
        stores.append(
            pltpu.make_async_copy(stage.at[:, span], down_out.at[0, :, span], sem.at[i])
        )
        stores[-1].start()
    for copy in stores + passes:
        copy.wait()


def shards(
    sizes,
    keys,
    values,
    queries,
    residual,
    out_proj,
    norm_gain,
    router,
    w_gate,
    w_up,
    w_down,
    head_vec,
    routes,
    step_pos,
    labels,
    trace_len,
):
    DP, SQ, EN = sizes
    G, E = DP * SQ, DP * EN
    N = G * EN
    width = residual.shape[2]
    WB = width // LANES
    hidden_units = w_gate.shape[2]
    hbm = pl.BlockSpec(memory_space=pl.ANY)
    message = (WB, LANES)
    operands = dict(
        queries=queries[0],
        step_pos=step_pos,
        trace_len=trace_len,
        keys=keys,
        values=values,
        residual=residual[0],
        norm_gain=norm_gain.reshape(message),
        router=router.T,
        head_vec=head_vec.reshape(message),
        routes=routes[0],
        labels=labels,
        out_proj=out_proj,
        w_gate=w_gate,
        w_up=w_up,
        w_down=w_down,
    )
    outs = dict(
        out_loss=jax.ShapeDtypeStruct((1, LANES), F32),
        out_hidden=jax.ShapeDtypeStruct((N, hidden_units), BF16),
        out_grads=jax.ShapeDtypeStruct((N, width), BF16),
        out_router=jax.ShapeDtypeStruct((E, width // N), BF16),
    )
    scratch = {
        name: pltpu.VMEM(operands[name].shape[-2:], operands[name].dtype) for name in INPUTS
    }
    scratch.update(
        loss=pltpu.VMEM((1, LANES), F32),
        hidden=pltpu.VMEM((N, hidden_units), BF16),
        grads=pltpu.VMEM((N, width), BF16),
        router_grad=pltpu.VMEM((E, width // N), BF16),
        q_own=pltpu.VMEM((QUERY_HEADS, LANES), BF16),
        q_buf=pltpu.VMEM((G, QUERY_HEADS, LANES), BF16),
        q_f32=pltpu.VMEM((G * QUERY_HEADS, LANES), F32),
        part_send=pltpu.VMEM((G, QUERY_HEADS + STAT_ROWS, LANES), BF16),
        part_buf=pltpu.VMEM((G, QUERY_HEADS + STAT_ROWS, LANES), BF16),
        mix_f32=pltpu.VMEM((G * WB, LANES), F32),
        mix_send=pltpu.VMEM((G,) + message, BF16),
        mix_buf=pltpu.VMEM((G,) + message, BF16),
        norm_own=pltpu.VMEM(message, BF16),
        norm_buf=pltpu.VMEM((N,) + message, BF16),
        norm_f32=pltpu.VMEM((N * WB, LANES), F32),
        rows=pltpu.VMEM((N, width), BF16),
        out_f32=pltpu.VMEM((N * WB, LANES), F32),
        half_send=pltpu.VMEM((SQ, E) + message, BF16),
        half_buf=pltpu.VMEM((SQ, E) + message, BF16),
        out_send=pltpu.VMEM((E,) + message, BF16),
        out_buf=pltpu.VMEM((E,) + message, BF16),
        grad_send=pltpu.VMEM((E,) + message, BF16),
        grad_buf=pltpu.VMEM((N,) + message, BF16),
        grad_f32=pltpu.VMEM((N * WB, LANES), F32),
        dlog_own=pltpu.VMEM((2, LANES), F32),
        dlog_buf=pltpu.VMEM((N, 2, LANES), F32),
        load_sem=pltpu.SemaphoreType.DMA((len(INPUTS),)),
        send_sem=pltpu.SemaphoreType.DMA((11,)),
        recv_sem=pltpu.SemaphoreType.DMA((11,)),
    )
    names = ["in_" + name for name in INPUTS] + list(outs) + list(scratch)
    loss, hidden, grads, grad_router = pl.pallas_call(
        functools.partial(kernel, sizes, names),
        out_shape=tuple(outs.values()),
        in_specs=[hbm] * len(INPUTS),
        out_specs=(hbm,) * len(outs),
        scratch_shapes=list(scratch.values()),
        compiler_params=pltpu.CompilerParams(
            collective_id=0, has_side_effects=True, vmem_limit_bytes=56 * 1024 * 1024
        ),
    )(*[operands[name] for name in INPUTS])
    loss, grad_down, grad_router = pl.pallas_call(
        down_kernel,
        out_shape=(
            jax.ShapeDtypeStruct((1, LANES), F32),
            jax.ShapeDtypeStruct((1, hidden_units, width), BF16),
            jax.ShapeDtypeStruct((E, width // N), BF16),
        ),
        in_specs=[hbm] * 4,
        out_specs=(hbm, hbm, hbm),
        scratch_shapes=[
            pltpu.VMEM((N, hidden_units), BF16),
            pltpu.VMEM((N, width), BF16),
            pltpu.VMEM((hidden_units, width), BF16),
            pltpu.SemaphoreType.DMA((8,)),
        ],
        compiler_params=pltpu.CompilerParams(vmem_limit_bytes=60 * 1024 * 1024),
    )(hidden, grads, loss, grad_router)
    return loss[0, 0], grad_down, grad_router.T


def solution(mesh):
    sizes = (mesh.shape["dp"], mesh.shape["seq"], mesh.shape["expert"])
    return jax.shard_map(
        functools.partial(shards, sizes),
        mesh=mesh,
        in_specs=(
            P("expert", ("dp", "seq"), None),
            P("expert", ("dp", "seq"), None),
            P("expert", ("dp", "seq"), None),
            P("expert", ("dp", "seq"), None),
            P(("dp", "seq"), None),
            P(),
            P(),
            P(("dp", "expert"), None, "seq"),
            P(("dp", "expert"), None, "seq"),
            P(("dp", "expert"), "seq", None),
            P(),
            P("expert", "dp", None),
            P("expert", None),
            P("expert", ("dp", "seq")),
            P("expert", None),
        ),
        out_specs=(P(), P(("dp", "expert"), "seq", None), P(("dp", "seq", "expert"), None)),
        check_vma=False,
    )
```

```python
import functools

import jax
import jax.numpy as jnp
from jax import lax
from jax.experimental import pallas as pl
from jax.experimental.pallas import tpu as pltpu
from jax.sharding import PartitionSpec as P

QUERY_HEADS = 32
KEY_VALUE_HEADS = 4
HEAD_WIDTH = 128
LANES = 128
MASKED = -1e30
EPSILON = 1e-06
STAT_ROWS = 16
INPUTS = (
    "queries",
    "step_pos",
    "trace_len",
    "keys",
    "values",
    "residual",
    "norm_gain",
    "router",
    "head_vec",
    "routes",
    "labels",
    "out_proj",
    "w_gate",
    "w_up",
    "w_down",
)
MESH = pl.DeviceIdType.MESH
F32 = jnp.float32
BF16 = jnp.bfloat16


def iota(shape, axis):
    return lax.broadcasted_iota(jnp.int32, shape, axis)


def total(x):
    return jnp.sum(jnp.sum(x, axis=1, keepdims=True), axis=0, keepdims=True)


def to_row(column, n):
    eye = iota((n, n), 0) == iota((n, n), 1)
    return jnp.sum(jnp.where(eye, column, 0.0), axis=0, keepdims=True)


def to_column(row, n):
    eye = iota((n, n), 0) == iota((n, n), 1)
    return jnp.sum(jnp.where(eye, row, 0.0), axis=1, keepdims=True)


def split3(x):
    high = x.astype(BF16).astype(F32)
    rest = x - high
    middle = rest.astype(BF16).astype(F32)
    return [high, middle, rest - middle]


def kernel(sizes, names, *refs):
    r = dict(zip(names, refs))
    DP, SQ, EN = sizes
    G, E = DP * SQ, DP * EN
    N = G * EN
    unroll = N <= 32
    proj_v, gate_v, up_v, down_v = r["out_proj"], r["w_gate"], r["w_up"], r["w_down"]
    width = proj_v.shape[1]
    WB = width // LANES
    dp, sq, ex = lax.axis_index("dp"), lax.axis_index("seq"), lax.axis_index("expert")
    mine = dp * SQ + sq
    expert = dp * EN + ex
    me = sq * E + expert
    tokens = r["keys"].shape[0]
    load_sem, send_sem, recv_sem = r["load_sem"], r["send_sem"], r["recv_sem"]

    loads = {}
    for i, name in enumerate(INPUTS):
        source, target = r["in_" + name], r[name]
        if len(source.shape) > len(target.shape):
            source = source.at[0]
        loads[name] = pltpu.make_async_copy(source, target, load_sem.at[i])
        loads[name].start()

    if unroll:
        near_dp = [lax.rem(dp + a, DP) for a in range(DP)]
        near_sq = [lax.rem(sq + a, SQ) for a in range(SQ)]
        near_ex = [lax.rem(ex + a, EN) for a in range(EN)]

        def near(a, b, c):
            return near_dp[a], near_sq[b], near_ex[c]
    else:

        def near(a, b, c):
            return lax.rem(dp + a, DP), lax.rem(sq + b, SQ), lax.rem(ex + c, EN)

    def each(first, last, body):
        if unroll:
            for i in range(first, last):
                body(i)
        else:

            def step(i, carry):
                body(i)
                return carry

            lax.fori_loop(first, last, step, 0)

    def to_pack(body):
        each(1, G, lambda i: body(near(i // SQ, i % SQ, 0)))

    def to_plane(body):
        each(1, E, lambda i: body(near(i // EN, 0, i % EN)))

    def to_all(body):
        each(1, N, lambda i: body(near(i // (SQ * EN), (i // EN) % SQ, i % EN)))

    def to_pair(body):
        each(1, SQ, lambda i: body(near(0, i, 0)))

    barrier = pltpu.get_barrier_semaphore()

    def greet(to):
        pl.semaphore_signal(barrier, inc=1, device_id=to, device_id_type=MESH)

    to_all(greet)

    def send(source, target, number, to):
        pltpu.make_async_remote_copy(
            src_ref=source,
            dst_ref=target,
            send_sem=send_sem.at[number],
            recv_sem=recv_sem.at[number],
            device_id=to,
            device_id_type=MESH,
        ).start()

    def await_all(buf, count, sem):
        span = buf.at[pl.ds(0, count)]
        pltpu.make_async_copy(span, span, sem).wait()

    q_own, q_buf, q_f32 = r["q_own"], r["q_buf"], r["q_f32"]
    loads["queries"].wait()
    q_row = r["queries"][...].astype(F32)
    q_own[...] = jnp.concatenate(
        [q_row[:, h * LANES : (h + 1) * LANES] for h in range(QUERY_HEADS)], axis=0
    ).astype(BF16)
    pl.semaphore_wait(barrier, N - 1)

    to_pack(lambda to: send(q_own, q_buf.at[mine], 0, to))
    q_buf[mine] = q_own[...]

    for name in INPUTS:
        if name not in ("queries", "out_proj", "w_gate", "w_up", "w_down"):
            loads[name].wait()
    traces = r["trace_len"].shape[1]
    pos_col = to_column(r["step_pos"][...].astype(F32), G)
    len_row = r["trace_len"][...].astype(F32)
    len_col = to_column(len_row, traces)
    before = iota((traces, traces), 0) <= iota((traces, traces), 1)
    ends_row = jnp.sum(jnp.where(before, len_col, 0.0), axis=0, keepdims=True)
    start_col = jnp.sum(jnp.where(ends_row <= pos_col, len_row, 0.0), axis=1, keepdims=True)
    key_pos = (mine * tokens + iota((G, tokens), 1)).astype(F32)
    allowed = jnp.where((key_pos <= pos_col) & (key_pos >= start_col), 1.0, 0.0)
    group = QUERY_HEADS // KEY_VALUE_HEADS
    allowed = jnp.concatenate([allowed] * group, axis=0) > 0.5
    await_all(q_buf, G - 1, recv_sem.at[0])

    part_send, part_buf = r["part_send"], r["part_buf"]
    key_v, value_v = r["keys"], r["values"]
    q_f32[...] = q_buf[...].astype(F32).reshape(G * QUERY_HEADS, LANES)
    peaks, sums = [], []
    owners = G // KEY_VALUE_HEADS
    for g in range(KEY_VALUE_HEADS):
        q_part = jnp.concatenate(
            [q_f32[pl.ds(g * group + h, G, stride=QUERY_HEADS), :] for h in range(group)], axis=0
        ).astype(BF16)
        columns = slice(g * HEAD_WIDTH, (g + 1) * HEAD_WIDTH)
        score = (
            lax.dot_general(
                q_part, key_v[:, columns], (((1,), (1,)), ((), ())), preferred_element_type=F32
            )
            * HEAD_WIDTH ** (-0.5)
        )
        score = jnp.where(allowed, score, MASKED)
        peak = jnp.max(score, axis=1, keepdims=True)
        weight = jnp.where(allowed, jnp.exp(score - peak), 0.0)
        peaks.append(peak)
        sums.append(jnp.sum(weight, axis=1, keepdims=True))
        part = jnp.dot(weight.astype(BF16), value_v[:, columns], preferred_element_type=F32)
        part_send[g * owners : (g + 1) * owners, 0:QUERY_HEADS] = part.astype(BF16).reshape(
            owners, QUERY_HEADS, LANES
        )
    peaks, sums = jnp.concatenate(peaks, axis=0), jnp.concatenate(sums, axis=0)
    per_block = LANES // QUERY_HEADS
    for b in range(G // per_block):
        span = slice(b * LANES, (b + 1) * LANES)
        stat = jnp.concatenate(
            split3(to_row(peaks[span], LANES))
            + split3(to_row(sums[span], LANES))
            + [jnp.zeros((STAT_ROWS - 6, LANES), F32)],
            axis=0,
        ).astype(BF16)
        part_send[b * per_block : (b + 1) * per_block, QUERY_HEADS:] = jnp.broadcast_to(
            stat[None], (per_block, STAT_ROWS, LANES)
        )

    to_pack(lambda to: send(part_send.at[to[0] * SQ + to[1]], part_buf.at[mine], 1, to))
    part_buf[mine] = part_send[mine]
    loads["out_proj"].wait()
    lane = iota((QUERY_HEADS, LANES), 1)
    pick = lane == lax.rem(mine, per_block) * QUERY_HEADS + iota((QUERY_HEADS, LANES), 0)
    await_all(part_buf, G - 1, recv_sem.at[1])

    stats = [part_buf[s, QUERY_HEADS:].astype(F32) for s in range(G)]
    peak_rows = jnp.concatenate([t[0:1] + t[1:2] + t[2:3] for t in stats], axis=0)
    sum_rows = jnp.concatenate([t[3:4] + t[4:5] + t[5:6] for t in stats], axis=0)
    factors = jnp.exp(peak_rows - jnp.max(peak_rows, axis=0, keepdims=True))
    factors = factors / jnp.sum(sum_rows * factors, axis=0, keepdims=True)
    attn = jnp.zeros((QUERY_HEADS, LANES), F32)
    for s in range(G):
        factor = jnp.sum(jnp.where(pick, factors[s : s + 1], 0.0), axis=1, keepdims=True)
        attn += part_buf[s, 0:QUERY_HEADS].astype(F32) * factor
    attn = jnp.concatenate(
        [attn[h * G : (h + 1) * G] for h in range(QUERY_HEADS // G)], axis=1
    ).astype(BF16)
    mixed = jnp.dot(attn, proj_v[...], preferred_element_type=F32)
    mix_f32, mix_send, mix_buf = r["mix_f32"], r["mix_send"], r["mix_buf"]
    for c in range(WB):
        mix_f32[pl.ds(c, G, stride=WB), :] = mixed[:, c * LANES : (c + 1) * LANES]
    mix_send[...] = mix_f32[...].astype(BF16).reshape(G, WB, LANES)

    to_pack(lambda to: send(mix_send.at[to[0] * SQ + to[1]], mix_buf.at[mine], 2, to))
    mix_buf[mine] = mix_send[mine]
    res_row = r["residual"][...].astype(F32)
    stream = jnp.concatenate(
        [res_row[:, c * LANES : (c + 1) * LANES] for c in range(WB)], axis=0
    )
    head_f32 = r["head_vec"][...].astype(F32)
    gain = r["norm_gain"][...].astype(F32)
    await_all(mix_buf, G - 1, recv_sem.at[2])
    stream += jnp.sum(mix_buf[...].astype(F32), axis=0)
    scale = lax.rsqrt(total(stream * stream) * (1.0 / width) + EPSILON)
    normed = (stream * scale * gain).astype(BF16)
    norm_own, norm_buf, norm_f32, rows = r["norm_own"], r["norm_buf"], r["norm_f32"], r["rows"]
    norm_own[...] = normed

    to_plane(lambda to: send(norm_own, norm_buf.at[me], 3, to))
    norm_buf[me] = norm_own[...]
    plane = pl.ds(sq * E, E)

    normed = normed.astype(F32)
    logits = jnp.zeros((E, LANES), F32)
    for c in range(WB):
        logits += r["router"][:, c * LANES : (c + 1) * LANES].astype(F32) * normed[c : c + 1]
    logits = jnp.sum(logits, axis=1, keepdims=True)
    route_row = r["routes"][pl.ds(sq, 1), :].astype(F32)
    topk = r["routes"].shape[1]
    chosen = jnp.sum(
        jnp.where(iota((E, topk), 0).astype(F32) == route_row, 1.0, 0.0), axis=1, keepdims=True
    )
    masked = jnp.where(chosen > 0.5, logits, MASKED)
    power = jnp.where(
        chosen > 0.5, jnp.exp(masked - jnp.max(masked, axis=0, keepdims=True)), 0.0
    )
    gate_weight = power / jnp.sum(power, axis=0, keepdims=True)

    await_all(norm_buf, E - 1, recv_sem.at[3])
    to_pair(lambda to: send(norm_buf.at[plane], norm_buf.at[plane], 4, to))
    for name in ("w_gate", "w_up", "w_down"):
        loads[name].wait()
    await_all(norm_buf, N - E, recv_sem.at[4])

    norm_f32[...] = norm_buf[...].astype(F32).reshape(N * WB, LANES)
    for c in range(WB):
        rows[:, c * LANES : (c + 1) * LANES] = norm_f32[pl.ds(c, N, stride=WB), :].astype(BF16)
    gate_act = jnp.dot(rows[...], gate_v[...], preferred_element_type=F32)
    up_act = jnp.dot(rows[...], up_v[...], preferred_element_type=F32)
    hidden = (gate_act / (1.0 + jnp.exp(-gate_act)) * up_act).astype(BF16)
    r["hidden"][...] = hidden
    stores = [pltpu.make_async_copy(r["hidden"], r["out_hidden"], load_sem.at[0])]
    stores[0].start()
    expert_out = jnp.dot(hidden, down_v[...], preferred_element_type=F32)
    out_f32, half_send, half_buf = r["out_f32"], r["half_send"], r["half_buf"]
    out_send, out_buf = r["out_send"], r["out_buf"]
    for c in range(WB):
        out_f32[pl.ds(c, N, stride=WB), :] = expert_out[:, c * LANES : (c + 1) * LANES]
    half_send[...] = out_f32[...].astype(BF16).reshape(SQ, E, WB, LANES)

    to_pair(lambda to: send(half_send.at[to[1]], half_buf.at[sq], 5, to))
    await_all(half_buf, SQ - 1, recv_sem.at[5])
    outs = out_f32[pl.ds(pl.multiple_of(sq * (E * WB), E * WB), E * WB), :].reshape(E, WB, LANES)
    for i in range(1, SQ):
        outs += half_buf[lax.rem(sq + i, SQ)].astype(F32)
    out_send[...] = outs.astype(BF16)
    to_plane(lambda to: send(out_send.at[to[0] * EN + to[2]], out_buf.at[expert], 6, to))
    out_buf[expert] = out_send[expert]
    own_label = r["labels"][...].astype(F32)
    weight_column = gate_weight.reshape(E, 1, 1)
    await_all(out_buf, E - 1, recv_sem.at[6])

    outs = out_buf[...].astype(F32)
    final = stream + jnp.sum(outs * weight_column, axis=0)
    scale = lax.rsqrt(total(final * final) * (1.0 / width) + EPSILON)
    along = total(final * head_f32)
    reward = along * scale
    decay = jnp.exp(-jnp.abs(reward))
    row_loss = jnp.maximum(reward, 0.0) + jnp.log1p(decay) - own_label * reward
    error = jnp.where(reward >= 0.0, 1.0, decay) / (1.0 + decay) - own_label
    d_mix = (
        (error * scale) * (head_f32 - final * (scale * scale * along * (1.0 / width)))
    ).astype(BF16).astype(F32)
    grad_send, grad_buf, grad_f32 = r["grad_send"], r["grad_buf"], r["grad_f32"]
    dlog_own, dlog_buf = r["dlog_own"], r["dlog_buf"]
    grad_send[...] = (weight_column * d_mix[None]).astype(BF16)

    to_all(lambda to: send(grad_send.at[to[0] * EN + to[2]], grad_buf.at[me], 7, to))
    grad_buf[me] = grad_send[expert]
    route_dot = jnp.sum(jnp.sum(outs * d_mix[None], axis=1), axis=1, keepdims=True)
    mean_dot = jnp.sum(gate_weight * route_dot, axis=0, keepdims=True)
    d_logits = to_row(gate_weight * (route_dot - mean_dot), E)
    if E < LANES:
        d_logits = jnp.concatenate([d_logits, jnp.zeros((1, LANES - E), F32)], axis=1)
    dlog_own[...] = jnp.concatenate(
        [d_logits, jnp.broadcast_to(row_loss, (1, LANES))], axis=0
    )
    to_all(lambda to: send(dlog_own, dlog_buf.at[me], 8, to))
    dlog_buf[me] = dlog_own[...]
    share = width // N
    first = (mine * EN + ex) * share
    own_columns = norm_f32[pl.ds(first // LANES, N, stride=WB), :]
    own_columns = pltpu.roll(own_columns, lax.rem(LANES - lax.rem(first, LANES), LANES), 1)

    await_all(grad_buf, N - 1, recv_sem.at[7])
    grad_f32[...] = grad_buf[...].astype(F32).reshape(N * WB, LANES)
    for c in range(WB):
        r["grads"][:, c * LANES : (c + 1) * LANES] = grad_f32[
            pl.ds(c, N, stride=WB), :
        ].astype(BF16)
    stores.append(pltpu.make_async_copy(r["grads"], r["out_grads"], load_sem.at[1]))
    stores[-1].start()
    await_all(dlog_buf, N - 1, recv_sem.at[8])
    r["loss"][...] = jnp.sum(dlog_buf[:, 1, :], axis=0, keepdims=True)
    router_grad = lax.dot_general(
        dlog_buf[:, 0, :],
        own_columns,
        (((0,), (0,)), ((), ())),
        precision=lax.Precision.HIGHEST,
        preferred_element_type=F32,
    )
    r["router_grad"][...] = router_grad[0:E, 0:share].astype(BF16)
    stores.append(pltpu.make_async_copy(r["loss"], r["out_loss"], load_sem.at[2]))
    stores[-1].start()
    stores.append(pltpu.make_async_copy(r["router_grad"], r["out_router"], load_sem.at[3]))
    stores[-1].start()

    for number, (buf, count) in enumerate(
        [
            (q_buf, G - 1),
            (part_buf, G - 1),
            (mix_buf, G - 1),
            (norm_buf, E - 1),
            (norm_buf, N - E),
            (half_buf, SQ - 1),
            (out_buf, E - 1),
            (grad_buf, N - 1),
            (dlog_buf, N - 1),
        ]
    ):
        await_all(buf, count, send_sem.at[number])
    for store in stores:
        store.wait()


def down_kernel(
    hidden, grads, loss, router_grad, loss_out, down_out, router_out, rows, columns, stage, sem
):
    loads = [
        pltpu.make_async_copy(hidden, rows, sem.at[4]),
        pltpu.make_async_copy(grads, columns, sem.at[5]),
    ]
    passes = [
        pltpu.make_async_copy(loss, loss_out, sem.at[6]),
        pltpu.make_async_copy(router_grad, router_out, sem.at[7]),
    ]
    for copy in loads + passes:
        copy.start()
    for load in loads:
        load.wait()
    step = stage.shape[1] // 4
    stores = []
    for i in range(4):
        span = pl.ds(i * step, step)
        stage[:, i * step : (i + 1) * step] = lax.dot_general(
            rows[...],
            columns[:, i * step : (i + 1) * step],
            (((0,), (0,)), ((), ())),
            preferred_element_type=F32,
        ).astype(BF16)
        stores.append(
            pltpu.make_async_copy(stage.at[:, span], down_out.at[0, :, span], sem.at[i])
        )
        stores[-1].start()
    for copy in stores + passes:
        copy.wait()


def shards(
    sizes,
    keys,
    values,
    queries,
    residual,
    out_proj,
    norm_gain,
    router,
    w_gate,
    w_up,
    w_down,
    head_vec,
    routes,
    step_pos,
    labels,
    trace_len,
):
    DP, SQ, EN = sizes
    G, E = DP * SQ, DP * EN
    N = G * EN
    width = residual.shape[2]
    WB = width // LANES
    hidden_units = w_gate.shape[2]
    hbm = pl.BlockSpec(memory_space=pl.ANY)
    message = (WB, LANES)
    operands = dict(
        queries=queries[0],
        step_pos=step_pos,
        trace_len=trace_len,
        keys=keys,
        values=values,
        residual=residual[0],
        norm_gain=norm_gain.reshape(message),
        router=router.T,
        head_vec=head_vec.reshape(message),
        routes=routes[0],
        labels=labels,
        out_proj=out_proj,
        w_gate=w_gate,
        w_up=w_up,
        w_down=w_down,
    )
    outs = dict(
        out_loss=jax.ShapeDtypeStruct((1, LANES), F32),
        out_hidden=jax.ShapeDtypeStruct((N, hidden_units), BF16),
        out_grads=jax.ShapeDtypeStruct((N, width), BF16),
        out_router=jax.ShapeDtypeStruct((E, width // N), BF16),
    )
    scratch = {
        name: pltpu.VMEM(operands[name].shape[-2:], operands[name].dtype) for name in INPUTS
    }
    scratch.update(
        loss=pltpu.VMEM((1, LANES), F32),
        hidden=pltpu.VMEM((N, hidden_units), BF16),
        grads=pltpu.VMEM((N, width), BF16),
        router_grad=pltpu.VMEM((E, width // N), BF16),
        q_own=pltpu.VMEM((QUERY_HEADS, LANES), BF16),
        q_buf=pltpu.VMEM((G, QUERY_HEADS, LANES), BF16),
        q_f32=pltpu.VMEM((G * QUERY_HEADS, LANES), F32),
        part_send=pltpu.VMEM((G, QUERY_HEADS + STAT_ROWS, LANES), BF16),
        part_buf=pltpu.VMEM((G, QUERY_HEADS + STAT_ROWS, LANES), BF16),
        mix_f32=pltpu.VMEM((G * WB, LANES), F32),
        mix_send=pltpu.VMEM((G,) + message, BF16),
        mix_buf=pltpu.VMEM((G,) + message, BF16),
        norm_own=pltpu.VMEM(message, BF16),
        norm_buf=pltpu.VMEM((N,) + message, BF16),
        norm_f32=pltpu.VMEM((N * WB, LANES), F32),
        rows=pltpu.VMEM((N, width), BF16),
        out_f32=pltpu.VMEM((N * WB, LANES), F32),
        half_send=pltpu.VMEM((SQ, E) + message, BF16),
        half_buf=pltpu.VMEM((SQ, E) + message, BF16),
        out_send=pltpu.VMEM((E,) + message, BF16),
        out_buf=pltpu.VMEM((E,) + message, BF16),
        grad_send=pltpu.VMEM((E,) + message, BF16),
        grad_buf=pltpu.VMEM((N,) + message, BF16),
        grad_f32=pltpu.VMEM((N * WB, LANES), F32),
        dlog_own=pltpu.VMEM((2, LANES), F32),
        dlog_buf=pltpu.VMEM((N, 2, LANES), F32),
        load_sem=pltpu.SemaphoreType.DMA((len(INPUTS),)),
        send_sem=pltpu.SemaphoreType.DMA((9,)),
        recv_sem=pltpu.SemaphoreType.DMA((9,)),
    )
    names = ["in_" + name for name in INPUTS] + list(outs) + list(scratch)
    loss, hidden, grads, grad_router = pl.pallas_call(
        functools.partial(kernel, sizes, names),
        out_shape=tuple(outs.values()),
        in_specs=[hbm] * len(INPUTS),
        out_specs=(hbm,) * len(outs),
        scratch_shapes=list(scratch.values()),
        compiler_params=pltpu.CompilerParams(
            collective_id=0, has_side_effects=True, vmem_limit_bytes=56 * 1024 * 1024
        ),
    )(*[operands[name] for name in INPUTS])
    loss, grad_down, grad_router = pl.pallas_call(
        down_kernel,
        out_shape=(
            jax.ShapeDtypeStruct((1, LANES), F32),
            jax.ShapeDtypeStruct((1, hidden_units, width), BF16),
            jax.ShapeDtypeStruct((E, width // N), BF16),
        ),
        in_specs=[hbm] * 4,
        out_specs=(hbm, hbm, hbm),
        scratch_shapes=[
            pltpu.VMEM((N, hidden_units), BF16),
            pltpu.VMEM((N, width), BF16),
            pltpu.VMEM((hidden_units, width), BF16),
            pltpu.SemaphoreType.DMA((8,)),
        ],
        compiler_params=pltpu.CompilerParams(vmem_limit_bytes=60 * 1024 * 1024),
    )(hidden, grads, loss, grad_router)
    return loss[0, 0], grad_down, grad_router.T


def solution(mesh):
    sizes = (mesh.shape["dp"], mesh.shape["seq"], mesh.shape["expert"])
    return jax.shard_map(
        functools.partial(shards, sizes),
        mesh=mesh,
        in_specs=(
            P("expert", ("dp", "seq"), None),
            P("expert", ("dp", "seq"), None),
            P("expert", ("dp", "seq"), None),
            P("expert", ("dp", "seq"), None),
            P(("dp", "seq"), None),
            P(),
            P(),
            P(("dp", "expert"), None, "seq"),
            P(("dp", "expert"), None, "seq"),
            P(("dp", "expert"), "seq", None),
            P(),
            P("expert", "dp", None),
            P("expert", None),
            P("expert", ("dp", "seq")),
            P("expert", None),
        ),
        out_specs=(P(), P(("dp", "expert"), "seq", None), P(("dp", "seq", "expert"), None)),
        check_vma=False,
    )
```
